32 devices in a mesh: doc: 16 (over z, y, x), qry: 2 (over core).
Axes of the slice: x: 2, y: 2, z: 4, core: 2. Of those that a mesh axis runs over, the one named last changes fastest.
Arguments:
- queries: bfloat16 [64, 4096], P('qry'), may hold values from -14 to 14
- passages: bfloat16 [4352, 4096], P(('doc', 'qry')), may hold values from -14 to 14
- passage_route: int32 [4352], P(('doc', 'qry')), may hold values from 0 to 8191, as said below
- pattern: int32 [2, 32], replicated, may hold values from 0 to 1, as said below
- teacher: float32 [64, 512], P(None, ('doc', 'qry')), may hold values from -20 to 270
Outputs:
- doc_scores: float32 [64, 512], P(None, ('doc', 'qry'))
- divergence: float32 [64], P('qry')
The draws below stay inside these ranges and needn't reach their ends.
Inputs may be any that keep to these rules, and one draw needn't show every extreme that they name: `passage_route`: A value v names document v // 16 (device g owns documents g * 16 to g * 16 + 15, with g = doc index * 2 + qry index) and passage v % 16 of it. Every document has 1 to 16 passages numbered from 0 without gaps, each held once over all shards, and its owner has the qry index of the shards that hold them. The passages of one owner are spread over the 16 shards of that qry index as evenly as possible (counts differ by at most one), so at most 16 go from one shard to one owner; in every qry index one owner holds 256 passages. Document t of the owner at doc index i and document t of the owner at doc index 15 - i, same qry index, have 16 + 1 passages together. `pattern`: entry [b, g] is 1 where queries b * 32 to b * 32 + 31 are scored against the documents of device g; every row has a 1.
All inputs are finite; a program needn't handle non-finite values.
Results may differ from the reference program's by a relative error of at most 0.0003.
Values may be sent and summed in bfloat16 or wider, within the bound.
No kernel may reach another device: no remote copies, remote signals or barrier semaphores. Data moves between devices by JAX's collectives and lax.ppermute only.
A program may use at most 64 MiB of HBM per device.

```python
import math
import jax
import jax.numpy as jnp
from jax import lax

D = 4096
MAXP = 16
QRY_DEV = 32
DOC_DEV = 16
PP = 136
NQ = 64
NDOC = 512
NP = 4352
N_DOC = 16
N_QRY = 2
DEVICES = 32


def route_table(key):
    base_key = jax.random.fold_in(key, 7001)
    keys = jax.random.split(base_key, 4)
    half_owners = N_DOC // 2
    shifts = jax.random.randint(keys[0], (N_QRY, half_owners, 1), -8, 9)
    hottest = jax.random.randint(keys[1], (N_QRY,), 0, half_owners)
    counts_low = jnp.clip(jax.random.randint(keys[2], (N_QRY, half_owners, DOC_DEV), 1, MAXP + 1) + shifts, 1, MAXP)
    owner_rank = jnp.arange(half_owners, dtype=jnp.int32)[None, :, None]
    counts_low = jnp.where(owner_rank == hottest[:, None, None], MAXP, counts_low)
    counts = jnp.concatenate([counts_low, (MAXP + 1 - counts_low)[:, ::-1, :]], axis=1)
    places = jnp.arange(MAXP, dtype=jnp.int32)[None, None, None, :]
    live = (places < counts[:, :, :, None]).astype(jnp.int32).reshape(N_QRY, -1)
    before = jnp.cumsum(live, axis=1) - live
    encoder_at = before % N_DOC
    local_at = before // N_DOC
    doc_index = jnp.arange(N_DOC, dtype=jnp.int32)[None, :, None, None]
    column_index = jnp.arange(N_QRY, dtype=jnp.int32)[:, None, None, None]
    within = jnp.arange(DOC_DEV, dtype=jnp.int32)[None, None, :, None]
    values = ((doc_index * N_QRY + column_index) * DOC_DEV + within) * MAXP + places
    values = jnp.broadcast_to(values, (N_QRY, N_DOC, DOC_DEV, MAXP)).reshape(N_QRY, -1)
    landing = jnp.where(live > 0, encoder_at * PP + local_at, N_DOC * PP)
    rows_of = jnp.arange(N_QRY, dtype=jnp.int32)[:, None]
    filled = jnp.zeros((N_QRY, N_DOC * PP + 1), jnp.int32).at[rows_of, landing].set(values)[:, :N_DOC * PP]
    filled = filled.reshape(N_QRY * N_DOC, PP)
    order_keys = jax.random.split(keys[3], N_QRY * N_DOC)
    orders = jax.vmap(lambda single: jax.random.permutation(single, PP))(order_keys)
    filled = jnp.take_along_axis(filled, orders, axis=1)
    filled = jnp.transpose(filled.reshape(N_QRY, N_DOC, PP), (1, 0, 2)).reshape(-1)
    return filled


def pattern_table(key):
    base_key = jax.random.fold_in(key, 7301)
    keys = jax.random.split(base_key, 2)
    entries = jax.random.randint(keys[0], (N_QRY, DEVICES), 0, 2)
    forced = jax.random.randint(keys[1], (N_QRY,), 0, DEVICES)
    return entries.at[jnp.arange(N_QRY), forced].set(1).astype(jnp.int32)


def passage_noise(key, row):
    row_key = jax.random.fold_in(jax.random.fold_in(key, 7101), row)
    values = jnp.clip(jax.random.normal(row_key, (D,), jnp.float32), -4.0, 4.0)
    return values


def draw_passages(key, part):
    rows = jnp.arange(NP, dtype=jnp.int32)
    noise = jax.vmap(lambda single: passage_noise(key, single))(rows)
    scales = jnp.exp(jax.random.uniform(jax.random.fold_in(key, 7103), (NP, 1), jnp.float32, math.log(0.6), math.log(2.5)))
    values = noise * scales
    return values.astype(jnp.bfloat16)


def draw_queries(key, part):
    keys = jax.random.split(jax.random.fold_in(key, 7201), 2)
    noise = jnp.clip(jax.random.normal(keys[0], (NQ, D), jnp.float32), -4.0, 4.0)
    scales = jnp.exp(jax.random.uniform(keys[1], (NQ, 1), jnp.float32, math.log(0.6), math.log(2.5)))
    values = noise * scales
    return values.astype(jnp.bfloat16)


def draw_passage_route(key, part):
    routes = route_table(key)
    return routes


def draw_pattern(key, part):
    return pattern_table(key)


def draw_teacher(key, part):
    keys = jax.random.split(jax.random.fold_in(key, 7401), 2)
    scales = jnp.exp(jax.random.uniform(keys[1], (NQ, 1), jnp.float32, math.log(0.5), math.log(5.0)))
    values = scales * jnp.clip(jax.random.normal(keys[0], (NQ, NDOC), jnp.float32), -4.0, 4.0)
    return values


def setup_inputs(seed: int = 0) -> dict:
    arg_keys = jax.random.split(jax.random.key(seed), 6)
    return {
        "queries": draw_queries(jax.random.fold_in(arg_keys[5], 71), 0),
        "passages": draw_passages(jax.random.fold_in(arg_keys[5], 71), 0),
        "passage_route": draw_passage_route(jax.random.fold_in(arg_keys[5], 71), 0),
        "pattern": draw_pattern(jax.random.fold_in(arg_keys[5], 71), 0),
        "teacher": draw_teacher(jax.random.fold_in(arg_keys[5], 71), 0),
    }


score_scale = 0.03125
very_negative = -1.0e30


def reference(queries, passages, passage_route, pattern, teacher):
    n_queries = queries.shape[0]
    n_docs = teacher.shape[1]
    n_passages = passages.shape[0]
    scores = lax.dot_general(queries, passages, (((1,), (1,)), ((), ())), preferred_element_type=jnp.float32) * score_scale
    inverse = jnp.full((n_docs * MAXP,), n_passages, jnp.int32).at[passage_route.astype(jnp.int32)].set(jnp.arange(n_passages, dtype=jnp.int32))
    inverse_blocks = inverse.reshape(n_docs // DOC_DEV, DOC_DEV * MAXP)

    def pool_owner(indices):
        picked = jnp.take(scores, indices, axis=1, mode="fill", fill_value=very_negative)
        masked = jnp.where((indices < n_passages)[None, :], picked, very_negative)
        masked = masked.reshape(n_queries, DOC_DEV, MAXP)
        highest = jnp.max(masked, axis=2)
        return highest + jnp.log(jnp.sum(jnp.exp(masked - highest[:, :, None]), axis=2))

    blocks = lax.map(pool_owner, inverse_blocks)
    pooled = jnp.transpose(blocks, (1, 0, 2)).reshape(n_queries, n_docs)
    active = jnp.repeat(jnp.repeat(pattern, QRY_DEV, axis=0), DOC_DEV, axis=1) > 0
    doc_scores = jnp.where(active, pooled, jnp.float32(0.0))
    peak_student = jnp.max(jnp.where(active, pooled, very_negative), axis=1)
    student_total = peak_student + jnp.log(jnp.sum(jnp.where(active, jnp.exp(pooled - peak_student[:, None]), jnp.float32(0.0)), axis=1))
    peak_teacher = jnp.max(jnp.where(active, teacher, very_negative), axis=1)
    teacher_total = peak_teacher + jnp.log(jnp.sum(jnp.where(active, jnp.exp(teacher - peak_teacher[:, None]), jnp.float32(0.0)), axis=1))
    probs = jnp.where(active, jnp.exp(teacher - teacher_total[:, None]), jnp.float32(0.0))
    divergence = jnp.sum(probs * (teacher - teacher_total[:, None] - pooled + student_total[:, None]), axis=1)
    return doc_scores, divergence
```

```python
import functools

import jax
import jax.numpy as jnp
from jax import lax
from jax.experimental import pallas as pl
from jax.experimental.pallas import tpu as pltpu
from jax.sharding import PartitionSpec as P

MAXP = 16
LANES = 128

score_scale = 0.03125
very_negative = -1e30

VMEM = pl.BlockSpec(memory_space=pltpu.VMEM)
SMEM = pl.BlockSpec(memory_space=pltpu.SMEM)
NT = (((1,), (1,)), ((), ()))


def dot_nt(a, b):
    return lax.dot_general(a, b, NT, preferred_element_type=jnp.float32)


def route_kernel(doc_count, capacity, table_rows, query_groups, route_ref, place_ref, ids_ref):
    rows = route_ref.shape[1]
    route = route_ref[...]
    owner = route // table_rows
    target = owner // query_groups
    slot = route - owner * table_rows
    down = lax.broadcasted_iota(jnp.int32, (rows, rows), 0)
    across = lax.broadcasted_iota(jnp.int32, (rows, rows), 1)

    def as_column(row):
        row = jnp.broadcast_to(row.astype(jnp.float32), (rows, rows))
        return jnp.sum(jnp.where(down == across, row, 0.0), axis=1, keepdims=True)

    target_row = target.astype(jnp.float32)
    target_column = as_column(target)
    earlier = (target_column == target_row) & (down < across)
    position = jnp.sum(jnp.where(earlier, 1.0, 0.0), axis=0, keepdims=True)
    placing = target_row * capacity + position
    outgoing = lax.broadcasted_iota(jnp.int32, (doc_count * capacity, rows), 0).astype(jnp.float32)
    place_ref[...] = jnp.where(outgoing == placing, 1.0, 0.0).astype(place_ref.dtype)
    ids_ref[...] = jnp.broadcast_to(as_column(slot) + 1.0, ids_ref.shape).astype(ids_ref.dtype)


def pack_kernel(own_first_ref, passages_ref, own_ref, *refs):
    other_refs, (place_ref, ids_ref, out_ref) = refs[:-3], refs[-3:]
    passages = passages_ref[...]
    logits = dot_nt(passages, own_ref[...])
    if other_refs:
        other = dot_nt(passages, other_refs[0][...])
        logits = jnp.where(
            own_first_ref[0] == 0,
            jnp.concatenate([logits, other], axis=1),
            jnp.concatenate([other, logits], axis=1),
        )
    logits = logits * score_scale
    high = logits.astype(jnp.bfloat16)
    low = (logits - high.astype(jnp.float32)).astype(jnp.bfloat16)
    everything = jnp.concatenate([high, low, ids_ref[...]], axis=1)
    out_ref[...] = jnp.dot(
        place_ref[...], everything, preferred_element_type=jnp.float32
    ).astype(out_ref.dtype)


def pool_kernel(rows_dev, query_groups, active_ref, arrived_ref, teacher_ref, scores_ref, out_ref):
    all_queries, doc_dev = teacher_ref.shape
    table_rows = doc_dev * MAXP
    arrived = arrived_ref[...]
    ids = arrived[:, 2 * all_queries :]
    first = jnp.where(lax.broadcasted_iota(jnp.int32, (8, LANES), 1) == 0, 1.0, 0.0)
    id_row = dot_nt(first.astype(jnp.bfloat16), ids)[:1]
    slots = lax.broadcasted_iota(jnp.int32, (table_rows, arrived.shape[0]), 0)
    wanted = (slots % doc_dev) * MAXP + slots // doc_dev + 1
    chosen = jnp.where(wanted.astype(jnp.float32) == id_row, 1.0, 0.0).astype(jnp.bfloat16)
    table = jnp.dot(chosen, arrived, preferred_element_type=jnp.float32)
    scores = table[:, :all_queries] + table[:, all_queries : 2 * all_queries]
    filled = table[:, 2 * all_queries :][:, :1] > 0.0
    masked = jnp.where(filled, scores, very_negative).reshape(MAXP, doc_dev, all_queries)
    highest = jnp.max(masked, axis=0)
    pooled = highest + jnp.log(jnp.sum(jnp.exp(masked - highest[None]), axis=0))
    lane = lax.broadcasted_iota(jnp.int32, (1, all_queries), 1)
    active = jnp.zeros((1, all_queries), jnp.bool_)
    for block in range(query_groups):
        inside = (lane >= block * rows_dev) & (lane < (block + 1) * rows_dev)
        active = active | (inside & (active_ref[block] > 0))
    scores_ref[...] = jnp.where(active, pooled, 0.0).T
    teacher = teacher_ref[...].T
    peak_student = jnp.max(pooled, axis=0, keepdims=True)
    student = peak_student + jnp.log(jnp.sum(jnp.exp(pooled - peak_student), axis=0, keepdims=True))
    peak_teacher = jnp.max(teacher, axis=0, keepdims=True)
    weights = jnp.exp(teacher - peak_teacher)
    weight_sum = jnp.sum(weights, axis=0, keepdims=True)
    mean = jnp.sum(weights * (teacher - pooled), axis=0, keepdims=True) / weight_sum
    student = jnp.where(active, student, very_negative)
    teacher_total = jnp.where(active, peak_teacher + jnp.log(weight_sum), very_negative)
    mean = jnp.where(active, mean, 0.0)
    lines = out_ref.shape[0]
    group = lax.broadcasted_iota(jnp.int32, out_ref.shape, 0) % query_groups
    out = jnp.zeros(out_ref.shape, jnp.float32)
    for block in range(query_groups):
        part = slice(block * rows_dev, (block + 1) * rows_dev)
        line = jnp.concatenate(
            [
                student[:, part],
                teacher_total[:, part],
                mean[:, part],
                jnp.zeros((1, out_ref.shape[1] - 3 * rows_dev), jnp.float32),
            ],
            axis=1,
        )
        out = jnp.where(group == block, jnp.broadcast_to(line, (lines, out_ref.shape[1])), out)
    out_ref[...] = out


def merge_kernel(rows_dev, parts_ref, out_ref):
    parts = parts_ref[...]
    student = parts[:, :rows_dev]
    teacher = parts[:, rows_dev : 2 * rows_dev]
    mean = parts[:, 2 * rows_dev : 3 * rows_dev]
    peak_student = jnp.max(student, axis=0, keepdims=True)
    student_total = peak_student + jnp.log(
        jnp.sum(jnp.exp(student - peak_student), axis=0, keepdims=True)
    )
    peak_teacher = jnp.max(teacher, axis=0, keepdims=True)
    weights = jnp.exp(teacher - peak_teacher)
    weight_sum = jnp.sum(weights, axis=0, keepdims=True)
    weighted = jnp.sum(weights * mean, axis=0, keepdims=True) / weight_sum
    out_ref[...] = weighted - (peak_teacher + jnp.log(weight_sum)) + student_total


def call(kernel, out_shape, in_specs, **cost):
    several = isinstance(out_shape, (list, tuple))
    return pl.pallas_call(
        kernel,
        out_shape=out_shape,
        in_specs=in_specs,
        out_specs=[VMEM] * len(out_shape) if several else VMEM,
        compiler_params=pltpu.CompilerParams(vmem_limit_bytes=16 * 1024 * 1024),
        cost_estimate=pl.CostEstimate(**cost) if cost else None,
    )


def on_device(queries, passages, passage_route, pattern, teacher):
    doc_count = lax.axis_size("doc")
    query_groups = lax.axis_size("qry")
    rows_dev, width = queries.shape
    rows = passages.shape[0]
    all_queries, doc_dev = teacher.shape
    table_rows = doc_dev * MAXP
    capacity = (table_rows + doc_count - 1) // doc_count
    core = lax.axis_index("qry")
    group_id = lax.axis_index("doc") * query_groups + core
    active = lax.dynamic_index_in_dim(pattern, group_id, 1, keepdims=False)

    if query_groups == 2:
        query_parts = [queries, lax.ppermute(queries, "qry", [(0, 1), (1, 0)])]
    else:
        query_parts = [lax.all_gather(queries, "qry", axis=0, tiled=True)]

    place, ids = call(
        functools.partial(route_kernel, doc_count, capacity, table_rows, query_groups),
        [
            jax.ShapeDtypeStruct((doc_count * capacity, rows), jnp.bfloat16),
            jax.ShapeDtypeStruct((rows, LANES), jnp.bfloat16),
        ],
        [VMEM],
        flops=rows * rows * 8,
        bytes_accessed=doc_count * capacity * rows * 2,
        transcendentals=0,
    )(passage_route.reshape(1, rows))
    outgoing = call(
        pack_kernel,
        jax.ShapeDtypeStruct((doc_count * capacity, 2 * all_queries + LANES), jnp.bfloat16),
        [SMEM] + [VMEM] * (len(query_parts) + 3),
    )(core.reshape(1), passages, *query_parts, place, ids)
    arrived = lax.all_to_all(outgoing, "doc", split_axis=0, concat_axis=0, tiled=True)
    line = -(-3 * rows_dev // LANES) * LANES
    devices = doc_count * query_groups
    doc_scores, partials = call(
        functools.partial(pool_kernel, rows_dev, query_groups),
        [
            jax.ShapeDtypeStruct((all_queries, doc_dev), jnp.float32),
            jax.ShapeDtypeStruct((devices, line), jnp.float32),
        ],
        [SMEM, VMEM, VMEM],
    )(active, arrived, teacher)
    everyone = lax.all_to_all(partials, ("doc", "qry"), split_axis=0, concat_axis=0, tiled=True)
    divergence = call(
        functools.partial(merge_kernel, rows_dev),
        jax.ShapeDtypeStruct((1, rows_dev), jnp.float32),
        [VMEM],
    )(everyone)
    return (doc_scores, divergence.reshape(rows_dev))


def solution(mesh):
    in_specs = (
        P("qry", None),
        P(("doc", "qry"), None),
        P(("doc", "qry")),
        P(),
        P(None, ("doc", "qry")),
    )
    out_specs = (P(None, ("doc", "qry")), P("qry"))
    return jax.shard_map(
        on_device, mesh=mesh, in_specs=in_specs, out_specs=out_specs, check_vma=False
    )
```

```python
import functools

import jax
import jax.numpy as jnp
from jax import lax
from jax.experimental import pallas as pl
from jax.experimental.pallas import tpu as pltpu
from jax.sharding import PartitionSpec as P

MAXP = 16
LANES = 128
SUBLANES = 8
CHUNKS = 4

score_scale = 0.03125
very_negative = -1e30

VMEM = pl.BlockSpec(memory_space=pltpu.VMEM)
HBM = pl.BlockSpec(memory_space=pltpu.HBM)
NT = (((1,), (1,)), ((), ()))


def dot_nt(a, b):
    return lax.dot_general(a, b, NT, preferred_element_type=jnp.float32)


def halves(logits):
    high = logits.astype(jnp.bfloat16)
    return high, (logits - high.astype(jnp.float32)).astype(jnp.bfloat16)


def before_kernel(
    sizes, passages_hbm, own_hbm, route_hbm, pattern_hbm, teacher_hbm,
    passages_ref, logits_ref, place_ref, ids_ref, weights_ref, notes_ref,
    own_ref, route_ref, pattern_ref, teacher_ref, passages_sem, small_sem,
):
    doc_count, query_groups, capacity, table_rows, rows_dev = sizes
    rows, width = passages_ref.shape
    step = width // CHUNKS
    copies = []
    for chunk in range(CHUNKS):
        part = pl.ds(chunk * step, step)
        copies.append(
            pltpu.make_async_copy(
                passages_hbm.at[:, part], passages_ref.at[:, part], passages_sem.at[chunk]
            )
        )
    small = [
        pltpu.make_async_copy(source, target, small_sem.at[k])
        for k, (source, target) in enumerate(
            [
                (route_hbm, route_ref),
                (pattern_hbm, pattern_ref),
                (teacher_hbm, teacher_ref),
                (own_hbm, own_ref),
            ]
        )
    ]
    for copy in small + copies:
        copy.start()
    core = lax.axis_index("qry")
    group_id = lax.axis_index("doc") * query_groups + core

    small[0].wait()
    route = route_ref[...]
    owner = route // table_rows
    target = (owner // query_groups).astype(jnp.float32)
    slot = (route - owner * table_rows).astype(jnp.float32)
    down = lax.broadcasted_iota(jnp.int32, (rows, rows), 0)
    across = lax.broadcasted_iota(jnp.int32, (rows, rows), 1)

    def as_column(row):
        row = jnp.broadcast_to(row, (rows, rows))
        return jnp.sum(jnp.where(down == across, row, 0.0), axis=1, keepdims=True)

    earlier = (as_column(target) == target) & (down < across)
    position = jnp.sum(jnp.where(earlier, 1.0, 0.0), axis=0, keepdims=True)
    placing = target * capacity + position
    outgoing = lax.broadcasted_iota(jnp.int32, (doc_count * capacity, rows), 0).astype(jnp.float32)
    place_ref[...] = jnp.where(outgoing == placing, 1.0, 0.0).astype(place_ref.dtype)
    ids_ref[...] = jnp.broadcast_to(as_column(slot) + 1.0, ids_ref.shape).astype(ids_ref.dtype)

    small[1].wait()
    all_queries = rows_dev * query_groups
    lane = lax.broadcasted_iota(jnp.int32, (1, all_queries), 1)
    mine = lax.broadcasted_iota(jnp.int32, pattern_ref.shape, 1) == group_id
    flags = jnp.sum(jnp.where(mine, pattern_ref[...], 0), axis=1, keepdims=True)
    active = jnp.zeros((1, all_queries), jnp.float32)
    for block in range(query_groups):
        inside = (lane >= block * rows_dev) & (lane < (block + 1) * rows_dev)
        flag = jnp.broadcast_to(flags[block : block + 1], (1, all_queries))
        active = jnp.where(inside & (flag > 0), 1.0, active)
    small[2].wait()
    teacher = teacher_ref[...]
    peak = jnp.max(teacher, axis=0, keepdims=True)
    weights = jnp.exp(teacher - peak)
    weight_sum = jnp.sum(weights, axis=0, keepdims=True)
    weights = weights / weight_sum
    weights_ref[...] = weights
    notes_ref[0:1, :] = jnp.where(active > 0.0, peak + jnp.log(weight_sum), very_negative)
    notes_ref[1:2, :] = jnp.sum(weights * teacher, axis=0, keepdims=True)
    notes_ref[2:3, :] = active
    notes_ref[3:4, :] = jnp.full((1, all_queries), core, jnp.int32).astype(jnp.float32)
    notes_ref[4:, :] = jnp.zeros((notes_ref.shape[0] - 4, all_queries), jnp.float32)

    small[3].wait()
    logits = jnp.zeros((rows, rows_dev), jnp.float32)
    for chunk in range(CHUNKS):
        part = pl.ds(chunk * step, step)
        copies[chunk].wait()
        logits += dot_nt(passages_ref[:, part], own_ref[:, part])
    logits_ref[...] = logits * score_scale


def pack_kernel(passages_ref, logits_ref, place_ref, ids_ref, *refs):
    other_refs, out_ref = refs[:-1], refs[-1]
    passages = passages_ref[...]
    parts = [halves(logits_ref[...])]
    parts += [halves(dot_nt(passages, other[...]) * score_scale) for other in other_refs]
    columns = [high for high, low in parts] + [low for high, low in parts] + [ids_ref[...]]
    out_ref[...] = jnp.dot(
        place_ref[...], jnp.concatenate(columns, axis=1), preferred_element_type=jnp.float32
    ).astype(out_ref.dtype)


def pool_kernel(rows_dev, query_groups, arrived_ref, weights_ref, notes_ref, scores_ref, out_ref):
    doc_dev, all_queries = weights_ref.shape
    table_rows = doc_dev * MAXP
    slots = arrived_ref.shape[0]
    first = jnp.where(lax.broadcasted_iota(jnp.int32, (SUBLANES, LANES), 1) == 0, 1.0, 0.0)
    id_row = dot_nt(first.astype(jnp.bfloat16), arrived_ref[:, 2 * all_queries :])[:1]
    shape = (MAXP, doc_dev, slots)
    wanted = lax.broadcasted_iota(jnp.int32, shape, 0) + lax.broadcasted_iota(jnp.int32, shape, 1) * MAXP
    wanted = wanted.reshape(table_rows, slots).astype(jnp.float32) + 1.0
    chosen = jnp.where(wanted == id_row, 1.0, 0.0).astype(jnp.bfloat16)
    table = jnp.dot(chosen, arrived_ref[:, : 2 * all_queries], preferred_element_type=jnp.float32)
    scores = table[:, :all_queries] + table[:, all_queries:]
    document = lax.broadcasted_iota(jnp.int32, (doc_dev, slots), 0).astype(jnp.float32)
    held = jnp.floor((id_row - 1.0) * (1.0 / MAXP)) == document
    count = jnp.sum(jnp.where(held, 1.0, 0.0), axis=1, keepdims=True)
    count = jnp.broadcast_to(count, (doc_dev, all_queries))
    scores = scores.reshape(MAXP, doc_dev, all_queries)
    places = [jnp.where(count > place, scores[place], very_negative) for place in range(MAXP)]
    highest = functools.reduce(jnp.maximum, places)
    total = functools.reduce(jnp.add, [jnp.exp(place - highest) for place in places])
    pooled = highest + jnp.log(total)
    if query_groups > 1:
        core = notes_ref[3:4, :]
        ordered = pooled
        for mine in range(1, query_groups):
            cut = all_queries - mine * rows_dev
            turned = jnp.concatenate([pooled[:, cut:], pooled[:, :cut]], axis=1)
            ordered = jnp.where(core == float(mine), turned, ordered)
        pooled = ordered
    active = notes_ref[2:3, :] > 0.0
    scores_ref[...] = jnp.where(active, pooled, 0.0)
    peak = jnp.max(pooled, axis=0, keepdims=True)
    student = peak + jnp.log(jnp.sum(jnp.exp(pooled - peak), axis=0, keepdims=True))
    student = jnp.where(active, student, very_negative)
    mean = notes_ref[1:2, :] - jnp.sum(weights_ref[...] * pooled, axis=0, keepdims=True)
    teacher = notes_ref[0:1, :]
    group = lax.broadcasted_iota(jnp.int32, out_ref.shape, 0) % query_groups
    out = jnp.zeros(out_ref.shape, jnp.float32)
    for block in range(query_groups):
        part = slice(block * rows_dev, (block + 1) * rows_dev)
        line = jnp.concatenate(
            [
                student[:, part],
                teacher[:, part],
                mean[:, part],
                jnp.zeros((1, out_ref.shape[1] - 3 * rows_dev), jnp.float32),
            ],
            axis=1,
        )
        out = jnp.where(group == block, jnp.broadcast_to(line, out_ref.shape), out)
    out_ref[...] = out


def merge_kernel(rows_dev, parts_ref, scores_in_ref, out_ref, scores_ref):
    scores_ref[...] = scores_in_ref[...]
    parts = parts_ref[...]
    student = parts[:, :rows_dev]
    teacher = parts[:, rows_dev : 2 * rows_dev]
    mean = parts[:, 2 * rows_dev : 3 * rows_dev]
    peak_student = jnp.max(student, axis=0, keepdims=True)
    student_total = peak_student + jnp.log(
        jnp.sum(jnp.exp(student - peak_student), axis=0, keepdims=True)
    )
    peak_teacher = jnp.max(teacher, axis=0, keepdims=True)
    weights = jnp.exp(teacher - peak_teacher)
    weight_sum = jnp.sum(weights, axis=0, keepdims=True)
    weighted = jnp.sum(weights * mean, axis=0, keepdims=True) / weight_sum
    out_ref[...] = weighted - (peak_teacher + jnp.log(weight_sum)) + student_total


def call(kernel, out_shape, in_specs, scratch=(), **cost):
    several = isinstance(out_shape, (list, tuple))
    return pl.pallas_call(
        kernel,
        out_shape=out_shape,
        in_specs=in_specs,
        out_specs=[VMEM] * len(out_shape) if several else VMEM,
        scratch_shapes=scratch,
        compiler_params=pltpu.CompilerParams(vmem_limit_bytes=16 * 1024 * 1024),
        cost_estimate=pl.CostEstimate(**cost) if cost else None,
    )


def on_device(queries, passages, passage_route, pattern, teacher):
    doc_count = lax.axis_size("doc")
    query_groups = lax.axis_size("qry")
    devices = doc_count * query_groups
    rows_dev, width = queries.shape
    rows = passages.shape[0]
    all_queries, doc_dev = teacher.shape
    table_rows = doc_dev * MAXP
    capacity = (table_rows + doc_count - 1) // doc_count
    f32, bf16 = jnp.float32, jnp.bfloat16
    shaped = jax.ShapeDtypeStruct

    others = [
        lax.ppermute(queries, "qry", [((i + k) % query_groups, i) for i in range(query_groups)])
        for k in range(1, query_groups)
    ]
    held, logits, place, ids, weights, notes = call(
        functools.partial(
            before_kernel, (doc_count, query_groups, capacity, table_rows, rows_dev)
        ),
        [
            shaped((rows, width), bf16),
            shaped((rows, rows_dev), f32),
            shaped((doc_count * capacity, rows), bf16),
            shaped((rows, LANES), bf16),
            shaped((doc_dev, all_queries), f32),
            shaped((SUBLANES, all_queries), f32),
        ],
        [HBM] * 5,
        [
            pltpu.VMEM((rows_dev, width), bf16),
            pltpu.VMEM((1, rows), jnp.int32),
            pltpu.VMEM(pattern.shape, jnp.int32),
            pltpu.VMEM((doc_dev, all_queries), f32),
            pltpu.SemaphoreType.DMA((CHUNKS,)),
            pltpu.SemaphoreType.DMA((4,)),
        ],
        flops=2 * rows * rows_dev * width,
        bytes_accessed=2 * (rows + rows_dev) * width,
        transcendentals=0,
    )(
        *[
            pltpu.with_memory_space_constraint(array, pltpu.HBM)
            for array in (passages, queries, passage_route.reshape(1, rows), pattern, teacher.T)
        ]
    )
    outgoing = call(
        pack_kernel,
        shaped((doc_count * capacity, 2 * all_queries + LANES), bf16),
        [VMEM] * (4 + len(others)),
    )(held, logits, place, ids, *others)
    arrived = lax.all_to_all(outgoing, "doc", split_axis=0, concat_axis=0, tiled=True)
    line = -(-3 * rows_dev // LANES) * LANES
    doc_scores, partials = call(
        functools.partial(pool_kernel, rows_dev, query_groups),
        [shaped((doc_dev, all_queries), f32), shaped((devices, line), f32)],
        [VMEM, VMEM, VMEM],
    )(arrived, weights, notes)
    everyone = lax.all_to_all(partials, ("doc", "qry"), split_axis=0, concat_axis=0, tiled=True)
    divergence, doc_scores = call(
        functools.partial(merge_kernel, rows_dev),
        [shaped((1, rows_dev), f32), shaped((doc_dev, all_queries), f32)],
        [VMEM, VMEM],
    )(everyone, doc_scores)
    return (doc_scores.T, divergence.reshape(rows_dev))


def solution(mesh):
    in_specs = (
        P("qry", None),
        P(("doc", "qry"), None),
        P(("doc", "qry")),
        P(),
        P(None, ("doc", "qry")),
    )
    out_specs = (P(None, ("doc", "qry")), P("qry"))
    return jax.shard_map(
        on_device, mesh=mesh, in_specs=in_specs, out_specs=out_specs, check_vma=False
    )
```

```python
import functools

import jax
import jax.numpy as jnp
from jax import lax
from jax.experimental import pallas as pl
from jax.experimental.pallas import tpu as pltpu
from jax.sharding import PartitionSpec as P

MAXP = 16
LANES = 128
SUBLANES = 8

score_scale = 0.03125
very_negative = -1e30

VMEM = pl.BlockSpec(memory_space=pltpu.VMEM)
HBM = pl.BlockSpec(memory_space=pltpu.HBM)
NT = (((1,), (1,)), ((), ()))


def dot_nt(a, b):
    return lax.dot_general(a, b, NT, preferred_element_type=jnp.float32)


def before_kernel(
    sizes, passages_hbm, own_hbm, route_hbm, pattern_hbm, teacher_hbm,
    passages_ref, own_ref, place_ref, ids_ref, weights_ref, notes_ref,
    route_ref, pattern_ref, teacher_ref, passages_sem, small_sem,
):
    doc_count, query_groups, capacity, table_rows, rows_dev = sizes
    rows = passages_ref.shape[0]
    pairs = [
        (route_hbm, route_ref),
        (pattern_hbm, pattern_ref),
        (teacher_hbm, teacher_ref),
        (own_hbm, own_ref),
    ]
    small = [
        pltpu.make_async_copy(source, target, small_sem.at[k])
        for k, (source, target) in enumerate(pairs)
    ]
    large = pltpu.make_async_copy(passages_hbm, passages_ref, passages_sem)
    small[0].start()
    large.start()
    for copy in small[1:]:
        copy.start()
    core = lax.axis_index("qry")
    group_id = lax.axis_index("doc") * query_groups + core

    small[0].wait()
    route = route_ref[...]
    owner = route // table_rows
    target = (owner // query_groups).astype(jnp.float32)
    slot = (route - owner * table_rows).astype(jnp.float32)
    down = lax.broadcasted_iota(jnp.int32, (rows, rows), 0)
    across = lax.broadcasted_iota(jnp.int32, (rows, rows), 1)

    def as_column(row):
        row = jnp.broadcast_to(row, (rows, rows))
        return jnp.sum(jnp.where(down == across, row, 0.0), axis=1, keepdims=True)

    earlier = (as_column(target) == target) & (down < across)
    position = jnp.sum(jnp.where(earlier, 1.0, 0.0), axis=0, keepdims=True)
    placing = target * capacity + position
    outgoing = lax.broadcasted_iota(jnp.int32, (doc_count * capacity, rows), 0).astype(jnp.float32)
    place_ref[...] = jnp.where(outgoing == placing, 1.0, 0.0).astype(place_ref.dtype)
    ids_ref[...] = jnp.broadcast_to(as_column(slot) + 1.0, ids_ref.shape).astype(ids_ref.dtype)

    small[1].wait()
    small[2].wait()
    all_queries = rows_dev * query_groups
    lane = lax.broadcasted_iota(jnp.int32, (1, all_queries), 1)
    mine = lax.broadcasted_iota(jnp.int32, pattern_ref.shape, 1) == group_id
    flags = jnp.sum(jnp.where(mine, pattern_ref[...], 0), axis=1, keepdims=True)
    active = jnp.zeros((1, all_queries), jnp.float32)
    for block in range(query_groups):
        inside = (lane >= block * rows_dev) & (lane < (block + 1) * rows_dev)
        flag = jnp.broadcast_to(flags[block : block + 1], (1, all_queries))
        active = jnp.where(inside & (flag > 0), 1.0, active)
    teacher = teacher_ref[...]
    peak = jnp.max(teacher, axis=0, keepdims=True)
    weights = jnp.exp(teacher - peak)
    weight_sum = jnp.sum(weights, axis=0, keepdims=True)
    weights = weights / weight_sum
    weights_ref[...] = weights
    notes_ref[0:1, :] = jnp.where(active > 0.0, peak + jnp.log(weight_sum), very_negative)
    notes_ref[1:2, :] = jnp.sum(weights * teacher, axis=0, keepdims=True)
    notes_ref[2:3, :] = active
    notes_ref[3:4, :] = jnp.full((1, all_queries), core, jnp.int32).astype(jnp.float32)
    notes_ref[4:, :] = jnp.zeros((notes_ref.shape[0] - 4, all_queries), jnp.float32)
    small[3].wait()
    large.wait()


def pack_kernel(passages_ref, place_ref, ids_ref, *refs):
    query_refs, out_ref = refs[:-1], refs[-1]
    queries = jnp.concatenate([part[...] for part in query_refs], axis=0)
    logits = dot_nt(passages_ref[...], queries) * score_scale
    high = logits.astype(jnp.bfloat16)
    low = (logits - high.astype(jnp.float32)).astype(jnp.bfloat16)
    columns = jnp.concatenate([high, low, ids_ref[...]], axis=1)
    out_ref[...] = jnp.dot(
        place_ref[...], columns, preferred_element_type=jnp.float32
    ).astype(out_ref.dtype)


def pool_kernel(rows_dev, query_groups, arrived_ref, weights_ref, notes_ref, scores_ref, out_ref):
    doc_dev, all_queries = weights_ref.shape
    table_rows = doc_dev * MAXP
    slots = arrived_ref.shape[0]
    first = jnp.where(lax.broadcasted_iota(jnp.int32, (SUBLANES, LANES), 1) == 0, 1.0, 0.0)
    id_row = dot_nt(first.astype(jnp.bfloat16), arrived_ref[:, 2 * all_queries :])[:1]
    shape = (MAXP, doc_dev, slots)
    wanted = lax.broadcasted_iota(jnp.int32, shape, 0) + lax.broadcasted_iota(jnp.int32, shape, 1) * MAXP
    wanted = wanted.reshape(table_rows, slots).astype(jnp.float32) + 1.0
    chosen = jnp.where(wanted == id_row, 1.0, 0.0).astype(jnp.bfloat16)
    table = jnp.dot(chosen, arrived_ref[:, : 2 * all_queries], preferred_element_type=jnp.float32)
    scores = table[:, :all_queries] + table[:, all_queries:]
    document = lax.broadcasted_iota(jnp.int32, (doc_dev, slots), 0).astype(jnp.float32)
    held = jnp.floor((id_row - 1.0) * (1.0 / MAXP)) == document
    count = jnp.sum(jnp.where(held, 1.0, 0.0), axis=1, keepdims=True)
    count = jnp.broadcast_to(count, (doc_dev, all_queries))
    scores = scores.reshape(MAXP, doc_dev, all_queries)
    places = [jnp.where(count > place, scores[place], very_negative) for place in range(MAXP)]
    highest = functools.reduce(jnp.maximum, places)
    total = functools.reduce(jnp.add, [jnp.exp(place - highest) for place in places])
    pooled = highest + jnp.log(total)
    if query_groups > 1:
        core = notes_ref[3:4, :]
        ordered = pooled
        for mine in range(1, query_groups):
            cut = all_queries - mine * rows_dev
            turned = jnp.concatenate([pooled[:, cut:], pooled[:, :cut]], axis=1)
            ordered = jnp.where(core == float(mine), turned, ordered)
        pooled = ordered
    active = notes_ref[2:3, :] > 0.0
    scores_ref[...] = jnp.where(active, pooled, 0.0)
    peak = jnp.max(pooled, axis=0, keepdims=True)
    student = peak + jnp.log(jnp.sum(jnp.exp(pooled - peak), axis=0, keepdims=True))
    student = jnp.where(active, student, very_negative)
    mean = notes_ref[1:2, :] - jnp.sum(weights_ref[...] * pooled, axis=0, keepdims=True)
    teacher = notes_ref[0:1, :]
    group = lax.broadcasted_iota(jnp.int32, out_ref.shape, 0) % query_groups
    out = jnp.zeros(out_ref.shape, jnp.float32)
    for block in range(query_groups):
        part = slice(block * rows_dev, (block + 1) * rows_dev)
        line = jnp.concatenate(
            [
                student[:, part],
                teacher[:, part],
                mean[:, part],
                jnp.zeros((1, out_ref.shape[1] - 3 * rows_dev), jnp.float32),
            ],
            axis=1,
        )
        out = jnp.where(group == block, jnp.broadcast_to(line, out_ref.shape), out)
    out_ref[...] = out


def merge_kernel(rows_dev, parts_ref, scores_in_ref, out_ref, scores_ref):
    scores_ref[...] = scores_in_ref[...]
    parts = parts_ref[...]
    student = parts[:, :rows_dev]
    teacher = parts[:, rows_dev : 2 * rows_dev]
    mean = parts[:, 2 * rows_dev : 3 * rows_dev]
    peak_student = jnp.max(student, axis=0, keepdims=True)
    student_total = peak_student + jnp.log(
        jnp.sum(jnp.exp(student - peak_student), axis=0, keepdims=True)
    )
    peak_teacher = jnp.max(teacher, axis=0, keepdims=True)
    weights = jnp.exp(teacher - peak_teacher)
    weight_sum = jnp.sum(weights, axis=0, keepdims=True)
    weighted = jnp.sum(weights * mean, axis=0, keepdims=True) / weight_sum
    out_ref[...] = weighted - (peak_teacher + jnp.log(weight_sum)) + student_total


def call(kernel, out_shape, in_specs, scratch=(), **cost):
    several = isinstance(out_shape, (list, tuple))
    return pl.pallas_call(
        kernel,
        out_shape=out_shape,
        in_specs=in_specs,
        out_specs=[VMEM] * len(out_shape) if several else VMEM,
        scratch_shapes=scratch,
        compiler_params=pltpu.CompilerParams(vmem_limit_bytes=16 * 1024 * 1024),
        cost_estimate=pl.CostEstimate(**cost) if cost else None,
    )


def on_device(queries, passages, passage_route, pattern, teacher):
    doc_count = lax.axis_size("doc")
    query_groups = lax.axis_size("qry")
    devices = doc_count * query_groups
    rows_dev, width = queries.shape
    rows = passages.shape[0]
    all_queries, doc_dev = teacher.shape
    table_rows = doc_dev * MAXP
    capacity = (table_rows + doc_count - 1) // doc_count
    f32, bf16 = jnp.float32, jnp.bfloat16
    shaped = jax.ShapeDtypeStruct

    others = [
        lax.ppermute(queries, "qry", [((i + k) % query_groups, i) for i in range(query_groups)])
        for k in range(1, query_groups)
    ]
    held, own, place, ids, weights, notes = call(
        functools.partial(
            before_kernel, (doc_count, query_groups, capacity, table_rows, rows_dev)
        ),
        [
            shaped((rows, width), bf16),
            shaped((rows_dev, width), bf16),
            shaped((doc_count * capacity, rows), bf16),
            shaped((rows, LANES), bf16),
            shaped((doc_dev, all_queries), f32),
            shaped((SUBLANES, all_queries), f32),
        ],
        [HBM] * 5,
        [
            pltpu.VMEM((1, rows), jnp.int32),
            pltpu.VMEM(pattern.shape, jnp.int32),
            pltpu.VMEM((doc_dev, all_queries), f32),
            pltpu.SemaphoreType.DMA(()),
            pltpu.SemaphoreType.DMA((4,)),
        ],
        flops=doc_count * capacity * rows,
        bytes_accessed=2 * (rows + rows_dev) * width,
        transcendentals=0,
    )(
        *[
            pltpu.with_memory_space_constraint(array, pltpu.HBM)
            for array in (passages, queries, passage_route.reshape(1, rows), pattern, teacher.T)
        ]
    )
    outgoing = call(
        pack_kernel,
        shaped((doc_count * capacity, 2 * all_queries + LANES), bf16),
        [VMEM] * (4 + len(others)),
    )(held, place, ids, own, *others)
    arrived = lax.all_to_all(outgoing, "doc", split_axis=0, concat_axis=0, tiled=True)
    line = -(-3 * rows_dev // LANES) * LANES
    doc_scores, partials = call(
        functools.partial(pool_kernel, rows_dev, query_groups),
        [shaped((doc_dev, all_queries), f32), shaped((devices, line), f32)],
        [VMEM, VMEM, VMEM],
    )(arrived, weights, notes)
    everyone = lax.all_to_all(partials, ("doc", "qry"), split_axis=0, concat_axis=0, tiled=True)
    divergence, doc_scores = call(
        functools.partial(merge_kernel, rows_dev),
        [shaped((1, rows_dev), f32), shaped((doc_dev, all_queries), f32)],
        [VMEM, VMEM],
    )(everyone, doc_scores)
    return (doc_scores.T, divergence.reshape(rows_dev))


def solution(mesh):
    in_specs = (
        P("qry", None),
        P(("doc", "qry"), None),
        P(("doc", "qry")),
        P(),
        P(None, ("doc", "qry")),
    )
    out_specs = (P(None, ("doc", "qry")), P("qry"))
    return jax.shard_map(
        on_device, mesh=mesh, in_specs=in_specs, out_specs=out_specs, check_vma=False
    )
```

```python
import functools

import jax
import jax.numpy as jnp
from jax import lax
from jax.experimental import pallas as pl
from jax.experimental.pallas import tpu as pltpu
from jax.sharding import PartitionSpec as P

MAXP = 16
LANES = 128
SUBLANES = 8

score_scale = 0.03125
very_negative = -1e30
tiny = 1e-30

STEPS = 10.0
LEVELS = 2.0 * STEPS + 1.0
STEP = 256.0 * STEPS

VMEM = pl.BlockSpec(memory_space=pltpu.VMEM)
HBM = pl.BlockSpec(memory_space=pltpu.HBM)
NT = (((1,), (1,)), ((), ()))


def turned(index, turn, size):
    index = index + turn % size
    return jnp.where(index >= size, index - size, index)


def turned_group(turn, size):
    return [[(k + turn) % size for k in range(size)]]


def dot_nt(a, b):
    return lax.dot_general(a, b, NT, preferred_element_type=jnp.float32)


def before_kernel(
    sizes, passages_hbm, own_hbm, route_hbm, pattern_hbm, teacher_hbm,
    passages_ref, own_ref, place_ref, ids_ref, weights_ref, notes_ref,
    route_ref, pattern_ref, teacher_ref, passages_sem, small_sem,
):
    doc_count, query_groups, capacity, table_rows, rows_dev, route_turn = sizes
    rows = passages_ref.shape[0]
    pairs = [
        (route_hbm, route_ref),
        (pattern_hbm, pattern_ref),
        (teacher_hbm, teacher_ref),
        (own_hbm, own_ref),
    ]
    small = [
        pltpu.make_async_copy(source, target, small_sem.at[k])
        for k, (source, target) in enumerate(pairs)
    ]
    large = pltpu.make_async_copy(passages_hbm, passages_ref, passages_sem)
    small[0].start()
    large.start()
    for copy in small[1:]:
        copy.start()
    core = lax.axis_index("qry")
    group_id = lax.axis_index("doc") * query_groups + core

    small[0].wait()
    route = route_ref[...]
    owner = route // table_rows
    target = turned(owner // query_groups, -route_turn, doc_count).astype(jnp.float32)
    slot = (route - owner * table_rows).astype(jnp.float32)
    down = lax.broadcasted_iota(jnp.int32, (rows, rows), 0)
    across = lax.broadcasted_iota(jnp.int32, (rows, rows), 1)

    def as_column(row):
        row = jnp.broadcast_to(row, (rows, rows))
        return jnp.sum(jnp.where(down == across, row, 0.0), axis=1, keepdims=True)

    earlier = (as_column(target) == target) & (down < across)
    position = jnp.sum(jnp.where(earlier, 1.0, 0.0), axis=0, keepdims=True)
    placing = target * capacity + position
    outgoing = lax.broadcasted_iota(jnp.int32, (doc_count * capacity, rows), 0).astype(jnp.float32)
    place_ref[...] = jnp.where(outgoing == placing, 1.0, 0.0).astype(place_ref.dtype)
    ids_ref[...] = jnp.broadcast_to(as_column(slot) + 1.0, ids_ref.shape).astype(ids_ref.dtype)

    small[1].wait()
    small[2].wait()
    all_queries = rows_dev * query_groups
    lane = lax.broadcasted_iota(jnp.int32, (1, all_queries), 1)
    mine = lax.broadcasted_iota(jnp.int32, pattern_ref.shape, 1) == group_id
    flags = jnp.sum(jnp.where(mine, pattern_ref[...], 0), axis=1, keepdims=True)
    active = jnp.zeros((1, all_queries), jnp.float32)
    for block in range(query_groups):
        inside = (lane >= block * rows_dev) & (lane < (block + 1) * rows_dev)
        flag = jnp.broadcast_to(flags[block : block + 1], (1, all_queries))
        active = jnp.where(inside & (flag > 0), 1.0, active)
    teacher = teacher_ref[...]
    peak = jnp.max(teacher, axis=0, keepdims=True)
    weights = jnp.exp(teacher - peak)
    weight_sum = jnp.sum(weights, axis=0, keepdims=True)
    weights = weights / weight_sum
    weights_ref[...] = weights
    notes_ref[0:1, :] = jnp.where(active > 0.0, peak + jnp.log(weight_sum), very_negative)
    notes_ref[1:2, :] = jnp.sum(weights * teacher, axis=0, keepdims=True)
    notes_ref[2:3, :] = active
    notes_ref[3:4, :] = jnp.full((1, all_queries), core, jnp.int32).astype(jnp.float32)
    notes_ref[4:, :] = jnp.zeros((notes_ref.shape[0] - 4, all_queries), jnp.float32)
    small[3].wait()
    large.wait()


def pack_kernel(passages_ref, place_ref, ids_ref, *refs):
    query_refs, out_ref = refs[:-1], refs[-1]
    queries = jnp.concatenate([part[...] for part in query_refs], axis=0)
    logits = dot_nt(passages_ref[...], queries) * score_scale
    count = logits.shape[1]
    high = logits.astype(jnp.bfloat16)
    rounded = high.astype(jnp.float32)
    low = logits - rounded
    inverse = pltpu.reciprocal(jnp.maximum(jnp.abs(rounded), tiny), approx=True)
    steps = jnp.floor(low * inverse * STEP + 0.5)
    steps = jnp.clip(steps, -STEPS, STEPS)
    shared = steps * LEVELS + jnp.concatenate([steps[:, 1:], steps[:, :1]], axis=1)
    lane = lax.broadcasted_iota(jnp.int32, logits.shape, 1)
    low = jnp.where(lane == count - 2, shared, low).astype(jnp.bfloat16)
    low = jnp.where(lane == count - 1, ids_ref[...], low)
    out_ref[...] = jnp.dot(
        place_ref[...], jnp.concatenate([high, low], axis=1), preferred_element_type=jnp.float32
    ).astype(out_ref.dtype)


def pool_kernel(rows_dev, query_groups, arrived_ref, weights_ref, notes_ref, scores_ref, out_ref):
    doc_dev, all_queries = weights_ref.shape
    table_rows = doc_dev * MAXP
    slots = arrived_ref.shape[0]
    columns = 2 * all_queries
    last = lax.broadcasted_iota(jnp.int32, (SUBLANES, columns), 1) == columns - 1
    last = jnp.where(last, 1.0, 0.0).astype(jnp.bfloat16)
    id_row = dot_nt(last, arrived_ref[...])[:1]
    shape = (MAXP, doc_dev, slots)
    wanted = lax.broadcasted_iota(jnp.int32, shape, 0) + lax.broadcasted_iota(jnp.int32, shape, 1) * MAXP
    wanted = wanted.reshape(table_rows, slots).astype(jnp.float32) + 1.0
    chosen = jnp.where(wanted == id_row, 1.0, 0.0).astype(jnp.bfloat16)
    table = jnp.dot(chosen, arrived_ref[...], preferred_element_type=jnp.float32)
    high, low = table[:, :all_queries], table[:, all_queries:]
    lane = lax.broadcasted_iota(jnp.int32, low.shape, 1)
    shared = jnp.where(lane == all_queries - 1, table[:, all_queries - 1 : columns - 1], low)
    steps = jnp.floor(shared * (1.0 / LEVELS) + 0.5)
    steps = jnp.where(lane == all_queries - 1, shared - LEVELS * steps, steps)
    scores = high + jnp.where(lane >= all_queries - 2, steps * jnp.abs(high) * (1.0 / STEP), low)
    document = lax.broadcasted_iota(jnp.int32, (doc_dev, slots), 0).astype(jnp.float32)
    held = jnp.floor((id_row - 1.0) * (1.0 / MAXP)) == document
    count = jnp.sum(jnp.where(held, 1.0, 0.0), axis=1, keepdims=True)
    count = jnp.broadcast_to(count, (doc_dev, all_queries))
    scores = scores.reshape(MAXP, doc_dev, all_queries)
    places = [jnp.where(count > place, scores[place], very_negative) for place in range(MAXP)]
    highest = functools.reduce(jnp.maximum, places)
    total = functools.reduce(jnp.add, [jnp.exp(place - highest) for place in places])
    pooled = highest + jnp.log(total)
    if query_groups > 1:
        core = notes_ref[3:4, :]
        ordered = pooled
        for mine in range(1, query_groups):
            cut = all_queries - mine * rows_dev
            shifted = jnp.concatenate([pooled[:, cut:], pooled[:, :cut]], axis=1)
            ordered = jnp.where(core == float(mine), shifted, ordered)
        pooled = ordered
    active = notes_ref[2:3, :] > 0.0
    scores_ref[...] = jnp.where(active, pooled, 0.0)
    peak = jnp.max(pooled, axis=0, keepdims=True)
    student = peak + jnp.log(jnp.sum(jnp.exp(pooled - peak), axis=0, keepdims=True))
    student = jnp.where(active, student, very_negative)
    mean = notes_ref[1:2, :] - jnp.sum(weights_ref[...] * pooled, axis=0, keepdims=True)
    teacher = notes_ref[0:1, :]
    group = lax.broadcasted_iota(jnp.int32, out_ref.shape, 0) % query_groups
    out = jnp.zeros(out_ref.shape, jnp.float32)
    for block in range(query_groups):
        part = slice(block * rows_dev, (block + 1) * rows_dev)
        line = jnp.concatenate(
            [
                student[:, part],
                teacher[:, part],
                mean[:, part],
                jnp.zeros((1, out_ref.shape[1] - 3 * rows_dev), jnp.float32),
            ],
            axis=1,
        )
        out = jnp.where(group == block, jnp.broadcast_to(line, out_ref.shape), out)
    out_ref[...] = out


def merge_kernel(rows_dev, parts_ref, scores_in_ref, out_ref, scores_ref):
    scores_ref[...] = scores_in_ref[...]
    parts = parts_ref[...]
    student = parts[:, :rows_dev]
    teacher = parts[:, rows_dev : 2 * rows_dev]
    mean = parts[:, 2 * rows_dev : 3 * rows_dev]
    peak_student = jnp.max(student, axis=0, keepdims=True)
    student_total = peak_student + jnp.log(
        jnp.sum(jnp.exp(student - peak_student), axis=0, keepdims=True)
    )
    peak_teacher = jnp.max(teacher, axis=0, keepdims=True)
    weights = jnp.exp(teacher - peak_teacher)
    weight_sum = jnp.sum(weights, axis=0, keepdims=True)
    weighted = jnp.sum(weights * mean, axis=0, keepdims=True) / weight_sum
    out_ref[...] = weighted - (peak_teacher + jnp.log(weight_sum)) + student_total


def call(kernel, out_shape, in_specs, scratch=(), **cost):
    several = isinstance(out_shape, (list, tuple))
    return pl.pallas_call(
        kernel,
        out_shape=out_shape,
        in_specs=in_specs,
        out_specs=[VMEM] * len(out_shape) if several else VMEM,
        scratch_shapes=scratch,
        compiler_params=pltpu.CompilerParams(vmem_limit_bytes=16 * 1024 * 1024),
        cost_estimate=pl.CostEstimate(**cost) if cost else None,
    )


def on_device(queries, passages, passage_route, pattern, teacher):
    doc_count = lax.axis_size("doc")
    query_groups = lax.axis_size("qry")
    devices = doc_count * query_groups
    rows_dev, width = queries.shape
    rows = passages.shape[0]
    all_queries, doc_dev = teacher.shape
    table_rows = doc_dev * MAXP
    capacity = (table_rows + doc_count - 1) // doc_count
    route_turn = doc_count // 4
    f32, bf16 = jnp.float32, jnp.bfloat16
    shaped = jax.ShapeDtypeStruct

    others = [
        lax.ppermute(queries, "qry", [((i + k) % query_groups, i) for i in range(query_groups)])
        for k in range(1, query_groups)
    ]
    held, own, place, ids, weights, notes = call(
        functools.partial(
            before_kernel,
            (doc_count, query_groups, capacity, table_rows, rows_dev, route_turn),
        ),
        [
            shaped((rows, width), bf16),
            shaped((rows_dev, width), bf16),
            shaped((doc_count * capacity, rows), bf16),
            shaped((rows, all_queries), bf16),
            shaped((doc_dev, all_queries), f32),
            shaped((SUBLANES, all_queries), f32),
        ],
        [HBM] * 5,
        [
            pltpu.VMEM((1, rows), jnp.int32),
            pltpu.VMEM(pattern.shape, jnp.int32),
            pltpu.VMEM((doc_dev, all_queries), f32),
            pltpu.SemaphoreType.DMA(()),
            pltpu.SemaphoreType.DMA((4,)),
        ],
        flops=doc_count * capacity * rows,
        bytes_accessed=2 * (rows + rows_dev) * width,
        transcendentals=0,
    )(
        *[
            pltpu.with_memory_space_constraint(array, pltpu.HBM)
            for array in (passages, queries, passage_route.reshape(1, rows), pattern, teacher.T)
        ]
    )
    outgoing = call(
        pack_kernel,
        shaped((doc_count * capacity, 2 * all_queries), bf16),
        [VMEM] * (4 + len(others)),
    )(held, place, ids, own, *others)
    arrived = lax.all_to_all(
        outgoing,
        "doc",
        split_axis=0,
        concat_axis=0,
        axis_index_groups=turned_group(route_turn, doc_count),
        tiled=True,
    )
    line = -(-3 * rows_dev // LANES) * LANES
    doc_scores, partials = call(
        functools.partial(pool_kernel, rows_dev, query_groups),
        [shaped((doc_dev, all_queries), f32), shaped((devices, line), f32)],
        [VMEM, VMEM, VMEM],
    )(arrived, weights, notes)
    everyone = lax.all_to_all(partials, ("doc", "qry"), split_axis=0, concat_axis=0, tiled=True)
    divergence, doc_scores = call(
        functools.partial(merge_kernel, rows_dev),
        [shaped((1, rows_dev), f32), shaped((doc_dev, all_queries), f32)],
        [VMEM, VMEM],
    )(everyone, doc_scores)
    return (doc_scores.T, divergence.reshape(rows_dev))


def solution(mesh):
    in_specs = (
        P("qry", None),
        P(("doc", "qry"), None),
        P(("doc", "qry")),
        P(),
        P(None, ("doc", "qry")),
    )
    out_specs = (P(None, ("doc", "qry")), P("qry"))
    return jax.shard_map(
        on_device, mesh=mesh, in_specs=in_specs, out_specs=out_specs, check_vma=False
    )
```

```python
import functools

import jax
import jax.numpy as jnp
from jax import lax
from jax.experimental import pallas as pl
from jax.experimental.pallas import tpu as pltpu
from jax.sharding import PartitionSpec as P

MAXP = 16
LANES = 128
SUBLANES = 8

score_scale = 0.03125
very_negative = -1e30
tiny = 1e-30

STEPS = 10.0
LEVELS = 2.0 * STEPS + 1.0
STEP = 256.0 * STEPS

VMEM = pl.BlockSpec(memory_space=pltpu.VMEM)
HBM = pl.BlockSpec(memory_space=pltpu.HBM)
NT = (((1,), (1,)), ((), ()))


def turned(index, turn, size):
    index = index + turn % size
    return jnp.where(index >= size, index - size, index)


def turned_group(turn, size):
    return [[(k + turn) % size for k in range(size)]]


def rolled(array, columns):
    if columns == 0:
        return array
    return jnp.concatenate([array[:, columns:], array[:, :columns]], axis=1)


def from_own(array, core, rows_dev, query_groups):
    out = array
    for mine in range(1, query_groups):
        out = jnp.where(core == mine, rolled(array, mine * rows_dev), out)
    return out


def from_first(array, core, rows_dev, query_groups):
    out = array
    for mine in range(1, query_groups):
        out = jnp.where(core == mine, rolled(array, (query_groups - mine) * rows_dev), out)
    return out


def dot_nt(a, b):
    return lax.dot_general(a, b, NT, preferred_element_type=jnp.float32)


def before_kernel(
    sizes, passages_hbm, own_hbm, route_hbm, pattern_hbm, teacher_hbm,
    passages_ref, own_ref, place_ref, ids_ref, weights_ref, notes_ref,
    route_ref, pattern_ref, teacher_ref, passages_sem, small_sem,
):
    doc_count, query_groups, capacity, table_rows, rows_dev, route_turn = sizes
    rows = passages_ref.shape[0]
    pairs = [
        (route_hbm, route_ref),
        (pattern_hbm, pattern_ref),
        (teacher_hbm, teacher_ref),
        (own_hbm, own_ref),
    ]
    small = [
        pltpu.make_async_copy(source, target, small_sem.at[k])
        for k, (source, target) in enumerate(pairs)
    ]
    large = pltpu.make_async_copy(passages_hbm, passages_ref, passages_sem)
    small[0].start()
    large.start()
    for copy in small[1:]:
        copy.start()
    core = lax.axis_index("qry")
    group_id = lax.axis_index("doc") * query_groups + core

    small[0].wait()
    route = route_ref[...]
    owner = route // table_rows
    target = turned(owner // query_groups, -route_turn, doc_count).astype(jnp.float32)
    slot = (route - owner * table_rows).astype(jnp.float32)
    down = lax.broadcasted_iota(jnp.int32, (rows, rows), 0)
    across = lax.broadcasted_iota(jnp.int32, (rows, rows), 1)

    def as_column(row):
        row = jnp.broadcast_to(row, (rows, rows))
        return jnp.sum(jnp.where(down == across, row, 0.0), axis=1, keepdims=True)

    earlier = (as_column(target) == target) & (down < across)
    position = jnp.sum(jnp.where(earlier, 1.0, 0.0), axis=0, keepdims=True)
    placing = target * capacity + position
    outgoing = lax.broadcasted_iota(jnp.int32, (doc_count * capacity, rows), 0).astype(jnp.float32)
    place_ref[...] = jnp.where(outgoing == placing, 1.0, 0.0).astype(place_ref.dtype)
    ids_ref[...] = jnp.broadcast_to(as_column(slot) + 1.0, ids_ref.shape).astype(ids_ref.dtype)

    small[1].wait()
    small[2].wait()
    all_queries = rows_dev * query_groups
    lane = lax.broadcasted_iota(jnp.int32, (1, all_queries), 1)
    mine = lax.broadcasted_iota(jnp.int32, pattern_ref.shape, 1) == group_id
    flags = jnp.sum(jnp.where(mine, pattern_ref[...], 0), axis=1, keepdims=True)
    active = jnp.zeros((1, all_queries), jnp.float32)
    for block in range(query_groups):
        inside = (lane >= block * rows_dev) & (lane < (block + 1) * rows_dev)
        flag = jnp.broadcast_to(flags[block : block + 1], (1, all_queries))
        active = jnp.where(inside & (flag > 0), 1.0, active)
    active = from_own(active, core, rows_dev, query_groups)
    teacher = from_own(teacher_ref[...], core, rows_dev, query_groups)
    peak = jnp.max(teacher, axis=0, keepdims=True)
    weights = jnp.exp(teacher - peak)
    weight_sum = jnp.sum(weights, axis=0, keepdims=True)
    weights = weights / weight_sum
    weights_ref[...] = weights
    notes_ref[0:1, :] = jnp.where(active > 0.0, peak + jnp.log(weight_sum), very_negative)
    notes_ref[1:2, :] = jnp.sum(weights * teacher, axis=0, keepdims=True)
    notes_ref[2:3, :] = active
    notes_ref[3:, :] = jnp.zeros((notes_ref.shape[0] - 3, all_queries), jnp.float32)
    small[3].wait()
    large.wait()


def pack_kernel(passages_ref, place_ref, ids_ref, *refs):
    query_refs, out_ref = refs[:-1], refs[-1]
    queries = jnp.concatenate([part[...] for part in query_refs], axis=0)
    logits = dot_nt(passages_ref[...], queries) * score_scale
    count = logits.shape[1]
    high = logits.astype(jnp.bfloat16)
    rounded = high.astype(jnp.float32)
    low = logits - rounded
    inverse = pltpu.reciprocal(jnp.maximum(jnp.abs(rounded), tiny), approx=True)
    steps = jnp.floor(low * inverse * STEP + 0.5)
    steps = jnp.clip(steps, -STEPS, STEPS)
    shared = steps * LEVELS + jnp.concatenate([steps[:, 1:], steps[:, :1]], axis=1)
    lane = lax.broadcasted_iota(jnp.int32, logits.shape, 1)
    low = jnp.where(lane == count - 2, shared, low).astype(jnp.bfloat16)
    low = jnp.where(lane == count - 1, ids_ref[...], low)
    out_ref[...] = jnp.dot(
        place_ref[...], jnp.concatenate([high, low], axis=1), preferred_element_type=jnp.float32
    ).astype(out_ref.dtype)


def pool_kernel(rows_dev, query_groups, arrived_ref, weights_ref, notes_ref, scores_ref, lines_ref):
    doc_dev, all_queries = weights_ref.shape
    table_rows = doc_dev * MAXP
    slots = arrived_ref.shape[0]
    columns = 2 * all_queries
    last = lax.broadcasted_iota(jnp.int32, (SUBLANES, columns), 1) == columns - 1
    last = jnp.where(last, 1.0, 0.0).astype(jnp.bfloat16)
    id_row = dot_nt(last, arrived_ref[...])[:1]
    shape = (MAXP, doc_dev, slots)
    wanted = lax.broadcasted_iota(jnp.int32, shape, 0) + lax.broadcasted_iota(jnp.int32, shape, 1) * MAXP
    wanted = wanted.reshape(table_rows, slots).astype(jnp.float32) + 1.0
    chosen = jnp.where(wanted == id_row, 1.0, 0.0).astype(jnp.bfloat16)
    table = jnp.dot(chosen, arrived_ref[...], preferred_element_type=jnp.float32)
    high, low = table[:, :all_queries], table[:, all_queries:]
    lane = lax.broadcasted_iota(jnp.int32, low.shape, 1)
    shared = jnp.where(lane == all_queries - 1, table[:, all_queries - 1 : columns - 1], low)
    steps = jnp.floor(shared * (1.0 / LEVELS) + 0.5)
    steps = jnp.where(lane == all_queries - 1, shared - LEVELS * steps, steps)
    scores = high + jnp.where(lane >= all_queries - 2, steps * jnp.abs(high) * (1.0 / STEP), low)
    document = lax.broadcasted_iota(jnp.int32, (doc_dev, slots), 0).astype(jnp.float32)
    held = jnp.floor((id_row - 1.0) * (1.0 / MAXP)) == document
    count = jnp.sum(jnp.where(held, 1.0, 0.0), axis=1, keepdims=True)
    count = jnp.broadcast_to(count, (doc_dev, all_queries))
    scores = scores.reshape(MAXP, doc_dev, all_queries)
    places = [jnp.where(count > place, scores[place], very_negative) for place in range(MAXP)]
    highest = functools.reduce(jnp.maximum, places)
    total = functools.reduce(jnp.add, [jnp.exp(place - highest) for place in places])
    pooled = highest + jnp.log(total)
    active = notes_ref[2:3, :] > 0.0
    scores_ref[...] = jnp.where(active, pooled, 0.0)
    peak = jnp.max(pooled, axis=0, keepdims=True)
    student = peak + jnp.log(jnp.sum(jnp.exp(pooled - peak), axis=0, keepdims=True))
    student = jnp.where(active, student, very_negative)
    mean = notes_ref[1:2, :] - jnp.sum(weights_ref[...] * pooled, axis=0, keepdims=True)
    teacher = notes_ref[0:1, :]
    row = lax.broadcasted_iota(jnp.int32, lines_ref.shape, 0)
    lines = jnp.zeros(lines_ref.shape, jnp.float32)
    for block in range(query_groups):
        part = slice(block * rows_dev, (block + 1) * rows_dev)
        line = jnp.concatenate(
            [
                student[:, part],
                teacher[:, part],
                mean[:, part],
                jnp.zeros((1, lines_ref.shape[1] - 3 * rows_dev), jnp.float32),
            ],
            axis=1,
        )
        lines = jnp.where(row == block, jnp.broadcast_to(line, lines_ref.shape), lines)
    lines_ref[...] = lines


def order_kernel(rows_dev, query_groups, scores_ref, out_ref):
    out_ref[...] = from_first(scores_ref[...], lax.axis_index("qry"), rows_dev, query_groups)


def spread_kernel(*refs):
    line_refs, out_ref = refs[:-1], refs[-1]
    sources = len(line_refs)
    source = lax.broadcasted_iota(jnp.int32, out_ref.shape, 0) % sources
    out = jnp.zeros(out_ref.shape, jnp.float32)
    for k, lines in enumerate(line_refs):
        part = (sources - k) % sources
        line = jnp.broadcast_to(lines[part : part + 1, :], out_ref.shape)
        out = jnp.where(source == k, line, out)
    out_ref[...] = out


def merge_kernel(rows_dev, parts_ref, out_ref):
    parts = parts_ref[...]
    student = parts[:, :rows_dev]
    teacher = parts[:, rows_dev : 2 * rows_dev]
    mean = parts[:, 2 * rows_dev : 3 * rows_dev]
    peak_student = jnp.max(student, axis=0, keepdims=True)
    student_total = peak_student + jnp.log(
        jnp.sum(jnp.exp(student - peak_student), axis=0, keepdims=True)
    )
    peak_teacher = jnp.max(teacher, axis=0, keepdims=True)
    weights = jnp.exp(teacher - peak_teacher)
    weight_sum = jnp.sum(weights, axis=0, keepdims=True)
    weighted = jnp.sum(weights * mean, axis=0, keepdims=True) / weight_sum
    out_ref[...] = weighted - (peak_teacher + jnp.log(weight_sum)) + student_total


def call(kernel, out_shape, in_specs, scratch=(), **cost):
    several = isinstance(out_shape, (list, tuple))
    return pl.pallas_call(
        kernel,
        out_shape=out_shape,
        in_specs=in_specs,
        out_specs=[VMEM] * len(out_shape) if several else VMEM,
        scratch_shapes=scratch,
        compiler_params=pltpu.CompilerParams(vmem_limit_bytes=16 * 1024 * 1024),
        cost_estimate=pl.CostEstimate(**cost) if cost else None,
    )


def from_others(array, query_groups):
    return [
        lax.ppermute(array, "qry", [((i + k) % query_groups, i) for i in range(query_groups)])
        for k in range(1, query_groups)
    ]


def on_device(queries, passages, passage_route, pattern, teacher):
    doc_count = lax.axis_size("doc")
    query_groups = lax.axis_size("qry")
    devices = doc_count * query_groups
    rows_dev, width = queries.shape
    rows = passages.shape[0]
    all_queries, doc_dev = teacher.shape
    table_rows = doc_dev * MAXP
    capacity = (table_rows + doc_count - 1) // doc_count
    route_turn = doc_count - 1
    total_turn = doc_count - 1
    f32, bf16 = jnp.float32, jnp.bfloat16
    shaped = jax.ShapeDtypeStruct

    others = from_others(queries, query_groups)
    held, own, place, ids, weights, notes = call(
        functools.partial(
            before_kernel,
            (doc_count, query_groups, capacity, table_rows, rows_dev, route_turn),
        ),
        [
            shaped((rows, width), bf16),
            shaped((rows_dev, width), bf16),
            shaped((doc_count * capacity, rows), bf16),
            shaped((rows, all_queries), bf16),
            shaped((doc_dev, all_queries), f32),
            shaped((SUBLANES, all_queries), f32),
        ],
        [HBM] * 5,
        [
            pltpu.VMEM((1, rows), jnp.int32),
            pltpu.VMEM(pattern.shape, jnp.int32),
            pltpu.VMEM((doc_dev, all_queries), f32),
            pltpu.SemaphoreType.DMA(()),
            pltpu.SemaphoreType.DMA((4,)),
        ],
        flops=doc_count * capacity * rows,
        bytes_accessed=2 * (rows + rows_dev) * width,
        transcendentals=0,
    )(
        *[
            pltpu.with_memory_space_constraint(array, pltpu.HBM)
            for array in (passages, queries, passage_route.reshape(1, rows), pattern, teacher.T)
        ]
    )
    outgoing = call(
        pack_kernel,
        shaped((doc_count * capacity, 2 * all_queries), bf16),
        [VMEM] * (4 + len(others)),
    )(held, place, ids, own, *others)
    arrived = lax.all_to_all(
        outgoing,
        "doc",
        split_axis=0,
        concat_axis=0,
        axis_index_groups=turned_group(route_turn, doc_count),
        tiled=True,
    )
    line = -(-3 * rows_dev // LANES) * LANES
    lines_rows = -(-query_groups // SUBLANES) * SUBLANES
    doc_scores, lines = call(
        functools.partial(pool_kernel, rows_dev, query_groups),
        [shaped((doc_dev, all_queries), f32), shaped((lines_rows, line), f32)],
        [VMEM, VMEM, VMEM],
    )(arrived, weights, notes)
    received = from_others(lines, query_groups)
    doc_scores = call(
        functools.partial(order_kernel, rows_dev, query_groups),
        shaped((doc_dev, all_queries), f32),
        [VMEM],
    )(doc_scores)
    doc_scores, received = lax.optimization_barrier((doc_scores, received))
    partials = call(spread_kernel, shaped((devices, line), f32), [VMEM] * query_groups)(
        lines, *received
    )
    everyone = lax.all_to_all(
        partials,
        "doc",
        split_axis=0,
        concat_axis=0,
        axis_index_groups=turned_group(total_turn, doc_count),
        tiled=True,
    )
    divergence = call(
        functools.partial(merge_kernel, rows_dev), shaped((1, rows_dev), f32), [VMEM]
    )(everyone)
    return (doc_scores.T, divergence.reshape(rows_dev))


def solution(mesh):
    in_specs = (
        P("qry", None),
        P(("doc", "qry"), None),
        P(("doc", "qry")),
        P(),
        P(None, ("doc", "qry")),
    )
    out_specs = (P(None, ("doc", "qry")), P("qry"))
    return jax.shard_map(
        on_device, mesh=mesh, in_specs=in_specs, out_specs=out_specs, check_vma=False
    )
```

```python
import functools
import random

import jax
import jax.numpy as jnp
from jax import lax
from jax.experimental import pallas as pl
from jax.experimental.pallas import tpu as pltpu
from jax.sharding import PartitionSpec as P

MAXP = 16
LANES = 128
SUBLANES = 8
ORDER_SEED = 3

score_scale = 0.03125
very_negative = -1e30
tiny = 1e-30

STEPS = 10.0
LEVELS = 2.0 * STEPS + 1.0
STEP = 256.0 * STEPS

VMEM = pl.BlockSpec(memory_space=pltpu.VMEM)
HBM = pl.BlockSpec(memory_space=pltpu.HBM)
NT = (((1,), (1,)), ((), ()))


def place_in(order, index):
    out = jnp.zeros(index.shape, jnp.int32)
    for place, entry in enumerate(order):
        out = jnp.where(index == entry, place, out)
    return out


def rolled(array, columns):
    if columns == 0:
        return array
    return jnp.concatenate([array[:, columns:], array[:, :columns]], axis=1)


def from_own(array, core, rows_dev, query_groups):
    out = array
    for mine in range(1, query_groups):
        out = jnp.where(core == mine, rolled(array, mine * rows_dev), out)
    return out


def from_first(array, core, rows_dev, query_groups):
    out = array
    for mine in range(1, query_groups):
        out = jnp.where(core == mine, rolled(array, (query_groups - mine) * rows_dev), out)
    return out


def dot_nt(a, b):
    return lax.dot_general(a, b, NT, preferred_element_type=jnp.float32)


def before_kernel(
    sizes, passages_hbm, own_hbm, route_hbm, pattern_hbm, teacher_hbm,
    passages_ref, own_ref, place_ref, ids_ref, weights_ref, notes_ref,
    route_ref, pattern_ref, teacher_ref, passages_sem, small_sem,
):
    doc_count, query_groups, capacity, table_rows, rows_dev, order = sizes
    rows = passages_ref.shape[0]
    pairs = [
        (route_hbm, route_ref),
        (pattern_hbm, pattern_ref),
        (teacher_hbm, teacher_ref),
        (own_hbm, own_ref),
    ]
    small = [
        pltpu.make_async_copy(source, target, small_sem.at[k])
        for k, (source, target) in enumerate(pairs)
    ]
    large = pltpu.make_async_copy(passages_hbm, passages_ref, passages_sem)
    small[0].start()
    large.start()
    for copy in small[1:]:
        copy.start()
    core = lax.axis_index("qry")
    group_id = lax.axis_index("doc") * query_groups + core

    small[0].wait()
    route = route_ref[...]
    owner = route // table_rows
    target = place_in(order, owner // query_groups).astype(jnp.float32)
    slot = (route - owner * table_rows).astype(jnp.float32)
    down = lax.broadcasted_iota(jnp.int32, (rows, rows), 0)
    across = lax.broadcasted_iota(jnp.int32, (rows, rows), 1)

    def as_column(row):
        row = jnp.broadcast_to(row, (rows, rows))
        return jnp.sum(jnp.where(down == across, row, 0.0), axis=1, keepdims=True)

    earlier = (as_column(target) == target) & (down < across)
    position = jnp.sum(jnp.where(earlier, 1.0, 0.0), axis=0, keepdims=True)
    placing = target * capacity + position
    outgoing = lax.broadcasted_iota(jnp.int32, (doc_count * capacity, rows), 0).astype(jnp.float32)
    place_ref[...] = jnp.where(outgoing == placing, 1.0, 0.0).astype(place_ref.dtype)
    ids_ref[...] = jnp.broadcast_to(as_column(slot) + 1.0, ids_ref.shape).astype(ids_ref.dtype)

    small[1].wait()
    small[2].wait()
    all_queries = rows_dev * query_groups
    lane = lax.broadcasted_iota(jnp.int32, (1, all_queries), 1)
    mine = lax.broadcasted_iota(jnp.int32, pattern_ref.shape, 1) == group_id
    flags = jnp.sum(jnp.where(mine, pattern_ref[...], 0), axis=1, keepdims=True)
    active = jnp.zeros((1, all_queries), jnp.float32)
    for block in range(query_groups):
        inside = (lane >= block * rows_dev) & (lane < (block + 1) * rows_dev)
        flag = jnp.broadcast_to(flags[block : block + 1], (1, all_queries))
        active = jnp.where(inside & (flag > 0), 1.0, active)
    active = from_own(active, core, rows_dev, query_groups)
    teacher = from_own(teacher_ref[...], core, rows_dev, query_groups)
    peak = jnp.max(teacher, axis=0, keepdims=True)
    weights = jnp.exp(teacher - peak)
    weight_sum = jnp.sum(weights, axis=0, keepdims=True)
    weights = weights / weight_sum
    weights_ref[...] = weights
    notes_ref[0:1, :] = jnp.where(active > 0.0, peak + jnp.log(weight_sum), very_negative)
    notes_ref[1:2, :] = jnp.sum(weights * teacher, axis=0, keepdims=True)
    notes_ref[2:3, :] = active
    notes_ref[3:, :] = jnp.zeros((notes_ref.shape[0] - 3, all_queries), jnp.float32)
    small[3].wait()
    large.wait()


def pack_kernel(passages_ref, place_ref, ids_ref, *refs):
    query_refs, out_ref = refs[:-1], refs[-1]
    queries = jnp.concatenate([part[...] for part in query_refs], axis=0)
    logits = dot_nt(passages_ref[...], queries) * score_scale
    count = logits.shape[1]
    high = logits.astype(jnp.bfloat16)
    rounded = high.astype(jnp.float32)
    low = logits - rounded
    inverse = pltpu.reciprocal(jnp.maximum(jnp.abs(rounded), tiny), approx=True)
    steps = jnp.floor(low * inverse * STEP + 0.5)
    steps = jnp.clip(steps, -STEPS, STEPS)
    shared = steps * LEVELS + jnp.concatenate([steps[:, 1:], steps[:, :1]], axis=1)
    lane = lax.broadcasted_iota(jnp.int32, logits.shape, 1)
    low = jnp.where(lane == count - 2, shared, low).astype(jnp.bfloat16)
    low = jnp.where(lane == count - 1, ids_ref[...], low)
    out_ref[...] = jnp.dot(
        place_ref[...], jnp.concatenate([high, low], axis=1), preferred_element_type=jnp.float32
    ).astype(out_ref.dtype)


def pool_kernel(rows_dev, query_groups, arrived_ref, weights_ref, notes_ref, scores_ref, lines_ref):
    doc_dev, all_queries = weights_ref.shape
    table_rows = doc_dev * MAXP
    slots = arrived_ref.shape[0]
    columns = 2 * all_queries
    last = lax.broadcasted_iota(jnp.int32, (SUBLANES, columns), 1) == columns - 1
    last = jnp.where(last, 1.0, 0.0).astype(jnp.bfloat16)
    id_row = dot_nt(last, arrived_ref[...])[:1]
    shape = (MAXP, doc_dev, slots)
    wanted = lax.broadcasted_iota(jnp.int32, shape, 0) + lax.broadcasted_iota(jnp.int32, shape, 1) * MAXP
    wanted = wanted.reshape(table_rows, slots).astype(jnp.float32) + 1.0
    chosen = jnp.where(wanted == id_row, 1.0, 0.0).astype(jnp.bfloat16)
    table = jnp.dot(chosen, arrived_ref[...], preferred_element_type=jnp.float32)
    high, low = table[:, :all_queries], table[:, all_queries:]
    lane = lax.broadcasted_iota(jnp.int32, low.shape, 1)
    shared = jnp.where(lane == all_queries - 1, table[:, all_queries - 1 : columns - 1], low)
    steps = jnp.floor(shared * (1.0 / LEVELS) + 0.5)
    steps = jnp.where(lane == all_queries - 1, shared - LEVELS * steps, steps)
    scores = high + jnp.where(lane >= all_queries - 2, steps * jnp.abs(high) * (1.0 / STEP), low)
    document = lax.broadcasted_iota(jnp.int32, (doc_dev, slots), 0).astype(jnp.float32)
    held = jnp.floor((id_row - 1.0) * (1.0 / MAXP)) == document
    count = jnp.sum(jnp.where(held, 1.0, 0.0), axis=1, keepdims=True)
    count = jnp.broadcast_to(count, (doc_dev, all_queries))
    scores = scores.reshape(MAXP, doc_dev, all_queries)
    places = [jnp.where(count > place, scores[place], very_negative) for place in range(MAXP)]
    highest = functools.reduce(jnp.maximum, places)
    total = functools.reduce(jnp.add, [jnp.exp(place - highest) for place in places])
    pooled = highest + jnp.log(total)
    active = notes_ref[2:3, :] > 0.0
    scores_ref[...] = jnp.where(active, pooled, 0.0)
    peak = jnp.max(pooled, axis=0, keepdims=True)
    student = peak + jnp.log(jnp.sum(jnp.exp(pooled - peak), axis=0, keepdims=True))
    student = jnp.where(active, student, very_negative)
    mean = notes_ref[1:2, :] - jnp.sum(weights_ref[...] * pooled, axis=0, keepdims=True)
    teacher = notes_ref[0:1, :]
    row = lax.broadcasted_iota(jnp.int32, lines_ref.shape, 0)
    lines = jnp.zeros(lines_ref.shape, jnp.float32)
    for block in range(query_groups):
        part = slice(block * rows_dev, (block + 1) * rows_dev)
        line = jnp.concatenate(
            [
                student[:, part],
                teacher[:, part],
                mean[:, part],
                jnp.zeros((1, lines_ref.shape[1] - 3 * rows_dev), jnp.float32),
            ],
            axis=1,
        )
        lines = jnp.where(row == block, jnp.broadcast_to(line, lines_ref.shape), lines)
    lines_ref[...] = lines


def order_kernel(rows_dev, query_groups, scores_ref, out_ref):
    out_ref[...] = from_first(scores_ref[...], lax.axis_index("qry"), rows_dev, query_groups)


def spread_kernel(first_place, *refs):
    line_refs, out_ref = refs[:-1], refs[-1]
    sources = len(line_refs)
    row = lax.broadcasted_iota(jnp.int32, out_ref.shape, 0)
    source = row % sources
    crossed = jnp.where(row // sources == first_place, 1, 0)
    here = jnp.where(lax.axis_index("doc") == 0, 1, 0)
    part = (crossed - here + sources) % sources
    out = jnp.zeros(out_ref.shape, jnp.float32)
    for k, lines in enumerate(line_refs):
        for ahead in range(sources):
            held = (ahead - k) % sources
            line = jnp.broadcast_to(lines[held : held + 1, :], out_ref.shape)
            out = jnp.where((source == k) & (part == ahead), line, out)
    out_ref[...] = out


def merge_kernel(rows_dev, parts_ref, out_ref):
    parts = parts_ref[...]
    student = parts[:, :rows_dev]
    teacher = parts[:, rows_dev : 2 * rows_dev]
    mean = parts[:, 2 * rows_dev : 3 * rows_dev]
    peak_student = jnp.max(student, axis=0, keepdims=True)
    student_total = peak_student + jnp.log(
        jnp.sum(jnp.exp(student - peak_student), axis=0, keepdims=True)
    )
    peak_teacher = jnp.max(teacher, axis=0, keepdims=True)
    weights = jnp.exp(teacher - peak_teacher)
    weight_sum = jnp.sum(weights, axis=0, keepdims=True)
    weighted = jnp.sum(weights * mean, axis=0, keepdims=True) / weight_sum
    out_ref[...] = weighted - (peak_teacher + jnp.log(weight_sum)) + student_total


def call(kernel, out_shape, in_specs, scratch=(), **cost):
    several = isinstance(out_shape, (list, tuple))
    return pl.pallas_call(
        kernel,
        out_shape=out_shape,
        in_specs=in_specs,
        out_specs=[VMEM] * len(out_shape) if several else VMEM,
        scratch_shapes=scratch,
        compiler_params=pltpu.CompilerParams(vmem_limit_bytes=16 * 1024 * 1024),
        cost_estimate=pl.CostEstimate(**cost) if cost else None,
    )


def crossed_groups(order, query_groups):
    return [
        [doc * query_groups + (core + (doc == 0)) % query_groups for doc in order]
        for core in range(query_groups)
    ]


def from_others(array, query_groups):
    return [
        lax.ppermute(array, "qry", [((i + k) % query_groups, i) for i in range(query_groups)])
        for k in range(1, query_groups)
    ]


def on_device(queries, passages, passage_route, pattern, teacher):
    doc_count = lax.axis_size("doc")
    query_groups = lax.axis_size("qry")
    devices = doc_count * query_groups
    rows_dev, width = queries.shape
    rows = passages.shape[0]
    all_queries, doc_dev = teacher.shape
    table_rows = doc_dev * MAXP
    capacity = (table_rows + doc_count - 1) // doc_count
    last_doc = doc_count - 1
    order = [last_doc] + random.Random(ORDER_SEED).sample(range(last_doc), last_doc)
    f32, bf16 = jnp.float32, jnp.bfloat16
    shaped = jax.ShapeDtypeStruct

    others = from_others(queries, query_groups)
    held, own, place, ids, weights, notes = call(
        functools.partial(
            before_kernel,
            (doc_count, query_groups, capacity, table_rows, rows_dev, order),
        ),
        [
            shaped((rows, width), bf16),
            shaped((rows_dev, width), bf16),
            shaped((doc_count * capacity, rows), bf16),
            shaped((rows, all_queries), bf16),
            shaped((doc_dev, all_queries), f32),
            shaped((SUBLANES, all_queries), f32),
        ],
        [HBM] * 5,
        [
            pltpu.VMEM((1, rows), jnp.int32),
            pltpu.VMEM(pattern.shape, jnp.int32),
            pltpu.VMEM((doc_dev, all_queries), f32),
            pltpu.SemaphoreType.DMA(()),
            pltpu.SemaphoreType.DMA((4,)),
        ],
        flops=doc_count * capacity * rows,
        bytes_accessed=2 * (rows + rows_dev) * width,
        transcendentals=0,
    )(
        *[
            pltpu.with_memory_space_constraint(array, pltpu.HBM)
            for array in (passages, queries, passage_route.reshape(1, rows), pattern, teacher.T)
        ]
    )
    outgoing = call(
        pack_kernel,
        shaped((doc_count * capacity, 2 * all_queries), bf16),
        [VMEM] * (4 + len(others)),
    )(held, place, ids, own, *others)
    arrived = lax.all_to_all(
        outgoing,
        "doc",
        split_axis=0,
        concat_axis=0,
        axis_index_groups=[order],
        tiled=True,
    )
    line = -(-3 * rows_dev // LANES) * LANES
    lines_rows = -(-query_groups // SUBLANES) * SUBLANES
    doc_scores, lines = call(
        functools.partial(pool_kernel, rows_dev, query_groups),
        [shaped((doc_dev, all_queries), f32), shaped((lines_rows, line), f32)],
        [VMEM, VMEM, VMEM],
    )(arrived, weights, notes)
    received = from_others(lines, query_groups)
    doc_scores = call(
        functools.partial(order_kernel, rows_dev, query_groups),
        shaped((doc_dev, all_queries), f32),
        [VMEM],
    )(doc_scores)
    doc_scores, received = lax.optimization_barrier((doc_scores, received))
    partials = call(
        functools.partial(spread_kernel, order.index(0)),
        shaped((devices, line), f32),
        [VMEM] * query_groups,
    )(lines, *received)
    everyone = lax.all_to_all(
        partials,
        ("doc", "qry"),
        split_axis=0,
        concat_axis=0,
        axis_index_groups=crossed_groups(order, query_groups),
        tiled=True,
    )
    divergence = call(
        functools.partial(merge_kernel, rows_dev), shaped((1, rows_dev), f32), [VMEM]
    )(everyone)
    return (doc_scores.T, divergence.reshape(rows_dev))


def solution(mesh):
    in_specs = (
        P("qry", None),
        P(("doc", "qry"), None),
        P(("doc", "qry")),
        P(),
        P(None, ("doc", "qry")),
    )
    out_specs = (P(None, ("doc", "qry")), P("qry"))
    return jax.shard_map(
        on_device, mesh=mesh, in_specs=in_specs, out_specs=out_specs, check_vma=False
    )
```

```python
import functools
import random

import jax
import jax.numpy as jnp
from jax import lax
from jax.experimental import pallas as pl
from jax.experimental.pallas import tpu as pltpu
from jax.sharding import PartitionSpec as P

MAXP = 16
LANES = 128
SUBLANES = 8
ORDER_SEED = 25

score_scale = 0.03125
very_negative = -1e30
tiny = 1e-30

STEPS = 10.0
LEVELS = 2.0 * STEPS + 1.0
STEP = 256.0 * STEPS

VMEM = pl.BlockSpec(memory_space=pltpu.VMEM)
HBM = pl.BlockSpec(memory_space=pltpu.HBM)
NT = (((1,), (1,)), ((), ()))


def place_in(order, index):
    out = jnp.zeros(index.shape, jnp.int32)
    for place, entry in enumerate(order):
        out = jnp.where(index == entry, place, out)
    return out


def rolled(array, columns):
    if columns == 0:
        return array
    return jnp.concatenate([array[:, columns:], array[:, :columns]], axis=1)


def from_own(array, core, rows_dev, query_groups):
    out = array
    for mine in range(1, query_groups):
        out = jnp.where(core == mine, rolled(array, mine * rows_dev), out)
    return out


def from_first(array, core, rows_dev, query_groups):
    out = array
    for mine in range(1, query_groups):
        out = jnp.where(core == mine, rolled(array, (query_groups - mine) * rows_dev), out)
    return out


def dot_nt(a, b):
    return lax.dot_general(a, b, NT, preferred_element_type=jnp.float32)


def before_kernel(
    sizes, passages_hbm, own_hbm, route_hbm, pattern_hbm, teacher_hbm,
    passages_ref, own_ref, place_ref, ids_ref, weights_ref, notes_ref,
    route_ref, pattern_ref, teacher_ref, passages_sem, small_sem,
):
    doc_count, query_groups, capacity, table_rows, rows_dev, order = sizes
    rows = passages_ref.shape[0]
    pairs = [
        (route_hbm, route_ref),
        (pattern_hbm, pattern_ref),
        (teacher_hbm, teacher_ref),
        (own_hbm, own_ref),
    ]
    small = [
        pltpu.make_async_copy(source, target, small_sem.at[k])
        for k, (source, target) in enumerate(pairs)
    ]
    large = pltpu.make_async_copy(passages_hbm, passages_ref, passages_sem)
    small[0].start()
    large.start()
    for copy in small[1:]:
        copy.start()
    core = lax.axis_index("qry")
    group_id = lax.axis_index("doc") * query_groups + core

    small[0].wait()
    route = route_ref[...]
    owner = route // table_rows
    target = place_in(order, owner // query_groups).astype(jnp.float32)
    slot = (route - owner * table_rows).astype(jnp.float32)
    down = lax.broadcasted_iota(jnp.int32, (rows, rows), 0)
    across = lax.broadcasted_iota(jnp.int32, (rows, rows), 1)

    def as_column(row):
        row = jnp.broadcast_to(row, (rows, rows))
        return jnp.sum(jnp.where(down == across, row, 0.0), axis=1, keepdims=True)

    earlier = (as_column(target) == target) & (down < across)
    position = jnp.sum(jnp.where(earlier, 1.0, 0.0), axis=0, keepdims=True)
    placing = target * capacity + position
    outgoing = lax.broadcasted_iota(jnp.int32, (doc_count * capacity, rows), 0).astype(jnp.float32)
    place_ref[...] = jnp.where(outgoing == placing, 1.0, 0.0).astype(place_ref.dtype)
    ids_ref[...] = jnp.broadcast_to(as_column(slot) + 1.0, ids_ref.shape).astype(ids_ref.dtype)

    small[1].wait()
    small[2].wait()
    all_queries = rows_dev * query_groups
    lane = lax.broadcasted_iota(jnp.int32, (1, all_queries), 1)
    mine = lax.broadcasted_iota(jnp.int32, pattern_ref.shape, 1) == group_id
    flags = jnp.sum(jnp.where(mine, pattern_ref[...], 0), axis=1, keepdims=True)
    active = jnp.zeros((1, all_queries), jnp.float32)
    for block in range(query_groups):
        inside = (lane >= block * rows_dev) & (lane < (block + 1) * rows_dev)
        flag = jnp.broadcast_to(flags[block : block + 1], (1, all_queries))
        active = jnp.where(inside & (flag > 0), 1.0, active)
    active = from_own(active, core, rows_dev, query_groups)
    teacher = from_own(teacher_ref[...], core, rows_dev, query_groups)
    peak = jnp.max(teacher, axis=0, keepdims=True)
    weights = jnp.exp(teacher - peak)
    weight_sum = jnp.sum(weights, axis=0, keepdims=True)
    weights = weights / weight_sum
    weights_ref[...] = weights
    notes_ref[0:1, :] = jnp.where(active > 0.0, peak + jnp.log(weight_sum), very_negative)
    notes_ref[1:2, :] = jnp.sum(weights * teacher, axis=0, keepdims=True)
    notes_ref[2:3, :] = active
    notes_ref[3:, :] = jnp.zeros((notes_ref.shape[0] - 3, all_queries), jnp.float32)
    small[3].wait()
    large.wait()


def pack_kernel(passages_ref, place_ref, ids_ref, *refs):
    query_refs, out_ref = refs[:-1], refs[-1]
    queries = jnp.concatenate([part[...] for part in query_refs], axis=0)
    logits = dot_nt(passages_ref[...], queries) * score_scale
    count = logits.shape[1]
    high = logits.astype(jnp.bfloat16)
    rounded = high.astype(jnp.float32)
    low = logits - rounded
    inverse = pltpu.reciprocal(jnp.maximum(jnp.abs(rounded), tiny), approx=True)
    steps = jnp.floor(low * inverse * STEP + 0.5)
    steps = jnp.clip(steps, -STEPS, STEPS)
    shared = steps * LEVELS + jnp.concatenate([steps[:, 1:], steps[:, :1]], axis=1)
    lane = lax.broadcasted_iota(jnp.int32, logits.shape, 1)
    low = jnp.where(lane == count - 2, shared, low).astype(jnp.bfloat16)
    low = jnp.where(lane == count - 1, ids_ref[...], low)
    out_ref[...] = jnp.dot(
        place_ref[...], jnp.concatenate([high, low], axis=1), preferred_element_type=jnp.float32
    ).astype(out_ref.dtype)


def pool_kernel(rows_dev, query_groups, arrived_ref, weights_ref, notes_ref, scores_ref, lines_ref):
    doc_dev, all_queries = weights_ref.shape
    table_rows = doc_dev * MAXP
    slots = arrived_ref.shape[0]
    columns = 2 * all_queries
    last = lax.broadcasted_iota(jnp.int32, (SUBLANES, columns), 1) == columns - 1
    last = jnp.where(last, 1.0, 0.0).astype(jnp.bfloat16)
    id_row = dot_nt(last, arrived_ref[...])[:1]
    shape = (MAXP, doc_dev, slots)
    wanted = lax.broadcasted_iota(jnp.int32, shape, 0) + lax.broadcasted_iota(jnp.int32, shape, 1) * MAXP
    wanted = wanted.reshape(table_rows, slots).astype(jnp.float32) + 1.0
    chosen = jnp.where(wanted == id_row, 1.0, 0.0).astype(jnp.bfloat16)
    table = jnp.dot(chosen, arrived_ref[...], preferred_element_type=jnp.float32)
    high, low = table[:, :all_queries], table[:, all_queries:]
    lane = lax.broadcasted_iota(jnp.int32, low.shape, 1)
    shared = jnp.where(lane == all_queries - 1, table[:, all_queries - 1 : columns - 1], low)
    steps = jnp.floor(shared * (1.0 / LEVELS) + 0.5)
    steps = jnp.where(lane == all_queries - 1, shared - LEVELS * steps, steps)
    scores = high + jnp.where(lane >= all_queries - 2, steps * jnp.abs(high) * (1.0 / STEP), low)
    document = lax.broadcasted_iota(jnp.int32, (doc_dev, slots), 0).astype(jnp.float32)
    held = jnp.floor((id_row - 1.0) * (1.0 / MAXP)) == document
    count = jnp.sum(jnp.where(held, 1.0, 0.0), axis=1, keepdims=True)
    count = jnp.broadcast_to(count, (doc_dev, all_queries))
    scores = scores.reshape(MAXP, doc_dev, all_queries)
    places = [jnp.where(count > place, scores[place], very_negative) for place in range(MAXP)]
    highest = functools.reduce(jnp.maximum, places)
    total = functools.reduce(jnp.add, [jnp.exp(place - highest) for place in places])
    pooled = highest + jnp.log(total)
    active = notes_ref[2:3, :] > 0.0
    scores_ref[...] = jnp.where(active, pooled, 0.0)
    peak = jnp.max(highest, axis=0, keepdims=True)
    student = peak + jnp.log(jnp.sum(total * jnp.exp(highest - peak), axis=0, keepdims=True))
    student = jnp.where(active, student, very_negative)
    mean = notes_ref[1:2, :] - jnp.sum(weights_ref[...] * pooled, axis=0, keepdims=True)
    teacher = notes_ref[0:1, :]
    row = lax.broadcasted_iota(jnp.int32, lines_ref.shape, 0)
    lines = jnp.zeros(lines_ref.shape, jnp.float32)
    for block in range(query_groups):
        part = slice(block * rows_dev, (block + 1) * rows_dev)
        line = jnp.concatenate(
            [
                student[:, part],
                teacher[:, part],
                mean[:, part],
                jnp.zeros((1, lines_ref.shape[1] - 3 * rows_dev), jnp.float32),
            ],
            axis=1,
        )
        lines = jnp.where(row == block, jnp.broadcast_to(line, lines_ref.shape), lines)
    lines_ref[...] = lines


def order_kernel(rows_dev, query_groups, scores_ref, out_ref):
    out_ref[...] = from_first(scores_ref[...], lax.axis_index("qry"), rows_dev, query_groups)


def spread_kernel(first_place, *refs):
    line_refs, out_ref = refs[:-1], refs[-1]
    sources = len(line_refs)
    row = lax.broadcasted_iota(jnp.int32, out_ref.shape, 0)
    source = row % sources
    crossed = jnp.where(row // sources == first_place, 1, 0)
    here = jnp.where(lax.axis_index("doc") == 0, 1, 0)
    part = (crossed - here + sources) % sources
    out = jnp.zeros(out_ref.shape, jnp.float32)
    for k, lines in enumerate(line_refs):
        for ahead in range(sources):
            held = (ahead - k) % sources
            line = jnp.broadcast_to(lines[held : held + 1, :], out_ref.shape)
            out = jnp.where((source == k) & (part == ahead), line, out)
    out_ref[...] = out


def merge_kernel(rows_dev, parts_ref, out_ref):
    parts = parts_ref[...]
    peak = jnp.max(parts, axis=0, keepdims=True)
    weights = jnp.exp(parts - peak)
    total = jnp.sum(weights, axis=0, keepdims=True)
    moved = jnp.concatenate([weights[:, -rows_dev:], weights[:, :-rows_dev]], axis=1)
    weighted = jnp.sum(moved * parts, axis=0, keepdims=True)
    totals = peak + jnp.log(total)
    columns = [slice(k * rows_dev, (k + 1) * rows_dev) for k in range(3)]
    out_ref[...] = (
        weighted[:, columns[2]] / total[:, columns[1]] - totals[:, columns[1]] + totals[:, columns[0]]
    )


def call(kernel, out_shape, in_specs, scratch=(), **cost):
    several = isinstance(out_shape, (list, tuple))
    return pl.pallas_call(
        kernel,
        out_shape=out_shape,
        in_specs=in_specs,
        out_specs=[VMEM] * len(out_shape) if several else VMEM,
        scratch_shapes=scratch,
        compiler_params=pltpu.CompilerParams(vmem_limit_bytes=16 * 1024 * 1024),
        cost_estimate=pl.CostEstimate(**cost) if cost else None,
    )


def crossed_groups(order, query_groups):
    return [
        [doc * query_groups + (core + (doc == 0)) % query_groups for doc in order]
        for core in range(query_groups)
    ]


def shuffled_from(first, size):
    others = [k for k in range(size) if k != first]
    return [first] + random.Random(ORDER_SEED).sample(others, size - 1)


def from_others(array, query_groups):
    return [
        lax.ppermute(array, "qry", [((i + k) % query_groups, i) for i in range(query_groups)])
        for k in range(1, query_groups)
    ]


def on_device(queries, passages, passage_route, pattern, teacher):
    doc_count = lax.axis_size("doc")
    query_groups = lax.axis_size("qry")
    devices = doc_count * query_groups
    rows_dev, width = queries.shape
    rows = passages.shape[0]
    all_queries, doc_dev = teacher.shape
    table_rows = doc_dev * MAXP
    capacity = (table_rows + doc_count - 1) // doc_count
    last_doc = doc_count - 1
    order = shuffled_from(last_doc, doc_count)
    route_order = shuffled_from(last_doc - doc_count // 4, doc_count)
    f32, bf16 = jnp.float32, jnp.bfloat16
    shaped = jax.ShapeDtypeStruct

    others = from_others(queries, query_groups)
    held, own, place, ids, weights, notes = call(
        functools.partial(
            before_kernel,
            (doc_count, query_groups, capacity, table_rows, rows_dev, route_order),
        ),
        [
            shaped((rows, width), bf16),
            shaped((rows_dev, width), bf16),
            shaped((doc_count * capacity, rows), bf16),
            shaped((rows, all_queries), bf16),
            shaped((doc_dev, all_queries), f32),
            shaped((SUBLANES, all_queries), f32),
        ],
        [HBM] * 5,
        [
            pltpu.VMEM((1, rows), jnp.int32),
            pltpu.VMEM(pattern.shape, jnp.int32),
            pltpu.VMEM((doc_dev, all_queries), f32),
            pltpu.SemaphoreType.DMA(()),
            pltpu.SemaphoreType.DMA((4,)),
        ],
        flops=doc_count * capacity * rows,
        bytes_accessed=2 * (rows + rows_dev) * width,
        transcendentals=0,
    )(
        *[
            pltpu.with_memory_space_constraint(array, pltpu.HBM)
            for array in (passages, queries, passage_route.reshape(1, rows), pattern, teacher.T)
        ]
    )
    outgoing = call(
        pack_kernel,
        shaped((doc_count * capacity, 2 * all_queries), bf16),
        [VMEM] * (4 + len(others)),
    )(held, place, ids, own, *others)
    arrived = lax.all_to_all(
        outgoing,
        "doc",
        split_axis=0,
        concat_axis=0,
        axis_index_groups=[route_order],
        tiled=True,
    )
    line = -(-3 * rows_dev // LANES) * LANES
    lines_rows = -(-query_groups // SUBLANES) * SUBLANES
    doc_scores, lines = call(
        functools.partial(pool_kernel, rows_dev, query_groups),
        [shaped((doc_dev, all_queries), f32), shaped((lines_rows, line), f32)],
        [VMEM, VMEM, VMEM],
    )(arrived, weights, notes)
    received = from_others(lines, query_groups)
    doc_scores = call(
        functools.partial(order_kernel, rows_dev, query_groups),
        shaped((doc_dev, all_queries), f32),
        [VMEM],
    )(doc_scores)
    doc_scores, received = lax.optimization_barrier((doc_scores, received))
    partials = call(
        functools.partial(spread_kernel, order.index(0)),
        shaped((devices, line), f32),
        [VMEM] * query_groups,
    )(lines, *received)
    everyone = lax.all_to_all(
        partials,
        ("doc", "qry"),
        split_axis=0,
        concat_axis=0,
        axis_index_groups=crossed_groups(order, query_groups),
        tiled=True,
    )
    divergence = call(
        functools.partial(merge_kernel, rows_dev), shaped((1, rows_dev), f32), [VMEM]
    )(everyone)
    return (doc_scores.T, divergence.reshape(rows_dev))


def solution(mesh):
    in_specs = (
        P("qry", None),
        P(("doc", "qry"), None),
        P(("doc", "qry")),
        P(),
        P(None, ("doc", "qry")),
    )
    out_specs = (P(None, ("doc", "qry")), P("qry"))
    return jax.shard_map(
        on_device, mesh=mesh, in_specs=in_specs, out_specs=out_specs, check_vma=False
    )
```

```python
import functools
import random

import jax
import jax.numpy as jnp
from jax import lax
from jax.experimental import pallas as pl
from jax.experimental.pallas import tpu as pltpu
from jax.sharding import PartitionSpec as P

MAXP = 16
LANES = 128
SUBLANES = 8
PACKED = 16
ORDER_SEED = 25

score_scale = 0.03125
very_negative = -1e30

VMEM = pl.BlockSpec(memory_space=pltpu.VMEM)
HBM = pl.BlockSpec(memory_space=pltpu.HBM)
NT = (((1,), (1,)), ((), ()))


def place_in(order, index):
    out = jnp.zeros(index.shape, jnp.int32)
    for place, entry in enumerate(order):
        out = jnp.where(index == entry, place, out)
    return out


def rolled(array, columns):
    if columns == 0:
        return array
    return jnp.concatenate([array[:, columns:], array[:, :columns]], axis=1)


def from_own(array, core, rows_dev, query_groups):
    out = array
    for mine in range(1, query_groups):
        out = jnp.where(core == mine, rolled(array, mine * rows_dev), out)
    return out


def from_first(array, core, rows_dev, query_groups):
    out = array
    for mine in range(1, query_groups):
        out = jnp.where(core == mine, rolled(array, (query_groups - mine) * rows_dev), out)
    return out


def dot_nt(a, b):
    return lax.dot_general(a, b, NT, preferred_element_type=jnp.float32)


def before_kernel(
    sizes, passages_hbm, own_hbm, route_hbm, pattern_hbm, teacher_hbm,
    passages_ref, own_ref, place_ref, ids_ref, weights_ref, notes_ref,
    route_ref, pattern_ref, teacher_ref, passages_sem, small_sem,
):
    doc_count, query_groups, capacity, table_rows, rows_dev, order = sizes
    rows = passages_ref.shape[0]
    pairs = [
        (route_hbm, route_ref),
        (pattern_hbm, pattern_ref),
        (teacher_hbm, teacher_ref),
        (own_hbm, own_ref),
    ]
    small = [
        pltpu.make_async_copy(source, target, small_sem.at[k])
        for k, (source, target) in enumerate(pairs)
    ]
    large = pltpu.make_async_copy(passages_hbm, passages_ref, passages_sem)
    small[0].start()
    large.start()
    for copy in small[1:]:
        copy.start()
    core = lax.axis_index("qry")
    group_id = lax.axis_index("doc") * query_groups + core

    small[0].wait()
    route = route_ref[...]
    owner = route // table_rows
    target = place_in(order, owner // query_groups).astype(jnp.float32)
    slot = (route - owner * table_rows).astype(jnp.float32)
    down = lax.broadcasted_iota(jnp.int32, (rows, rows), 0)
    across = lax.broadcasted_iota(jnp.int32, (rows, rows), 1)

    def as_column(row):
        row = jnp.broadcast_to(row, (rows, rows))
        return jnp.sum(jnp.where(down == across, row, 0.0), axis=1, keepdims=True)

    earlier = (as_column(target) == target) & (down < across)
    position = jnp.sum(jnp.where(earlier, 1.0, 0.0), axis=0, keepdims=True)
    placing = target * capacity + position
    outgoing = lax.broadcasted_iota(jnp.int32, (doc_count * capacity, rows), 0).astype(jnp.float32)
    place_ref[...] = jnp.where(outgoing == placing, 1.0, 0.0).astype(place_ref.dtype)
    columns = ids_ref.shape[1]
    mine = place_in(order, jnp.full((1, 1), lax.axis_index("doc"), jnp.int32)) * capacity
    arriving = as_column(position) + mine.astype(jnp.float32)
    number = as_column(slot) + 1.0
    row = lax.broadcasted_iota(jnp.int32, (ids_ref.shape[0], rows), 0)
    column = lax.broadcasted_iota(jnp.int32, (rows, columns), 1).astype(jnp.float32)
    ids = jnp.zeros(ids_ref.shape, jnp.float32)
    for line in range(-(-doc_count * capacity // columns)):
        goes = ((row // SUBLANES).astype(jnp.float32) == target) & (row % SUBLANES == line)
        goes = jnp.where(goes, 1.0, 0.0).astype(jnp.bfloat16)
        here = jnp.where(column + float(line * columns) == arriving, number, 0.0)
        ids += jnp.dot(goes, here.astype(jnp.bfloat16), preferred_element_type=jnp.float32)
    ids_ref[...] = ids

    small[1].wait()
    small[2].wait()
    all_queries = rows_dev * query_groups
    lane = lax.broadcasted_iota(jnp.int32, (1, all_queries), 1)
    own = lax.broadcasted_iota(jnp.int32, pattern_ref.shape, 1) == group_id
    flags = jnp.sum(jnp.where(own, pattern_ref[...], 0), axis=1, keepdims=True)
    active = jnp.zeros((1, all_queries), jnp.float32)
    for block in range(query_groups):
        inside = (lane >= block * rows_dev) & (lane < (block + 1) * rows_dev)
        flag = jnp.broadcast_to(flags[block : block + 1], (1, all_queries))
        active = jnp.where(inside & (flag > 0), 1.0, active)
    active = from_own(active, core, rows_dev, query_groups)
    teacher = from_own(teacher_ref[...], core, rows_dev, query_groups)
    peak = jnp.max(teacher, axis=0, keepdims=True)
    weights = jnp.exp(teacher - peak)
    weight_sum = jnp.sum(weights, axis=0, keepdims=True)
    weights = weights / weight_sum
    weights_ref[...] = weights
    notes_ref[0:1, :] = jnp.where(active > 0.0, peak + jnp.log(weight_sum), very_negative)
    notes_ref[1:2, :] = jnp.sum(weights * teacher, axis=0, keepdims=True)
    notes_ref[2:3, :] = active
    notes_ref[3:, :] = jnp.zeros((notes_ref.shape[0] - 3, all_queries), jnp.float32)
    small[3].wait()
    large.wait()


def pack_kernel(passages_ref, place_ref, ids_ref, *refs):
    query_refs, out_ref = refs[:-1], refs[-1]
    doc_count, block_rows, columns = out_ref.shape
    capacity = block_rows - SUBLANES
    queries = jnp.concatenate([part[...] for part in query_refs], axis=0)
    logits = dot_nt(passages_ref[...], queries) * score_scale
    high = logits.astype(jnp.bfloat16)
    low = (logits - high.astype(jnp.float32)).astype(jnp.bfloat16)
    placed = jnp.dot(
        place_ref[...], jnp.concatenate([high, low], axis=1), preferred_element_type=jnp.float32
    )
    out_ref[:, :capacity, :] = placed.reshape(doc_count, capacity, columns).astype(out_ref.dtype)
    ids = ids_ref[...].reshape(doc_count, SUBLANES, columns)
    out_ref[:, capacity:, :] = ids.astype(out_ref.dtype)


def pool_kernel(rows_dev, query_groups, arrived_ref, weights_ref, notes_ref, scores_ref, lines_ref):
    doc_dev, all_queries = weights_ref.shape
    table_rows = doc_dev * MAXP
    doc_count, block_rows, columns = arrived_ref.shape
    capacity = block_rows - SUBLANES
    slots = doc_count * capacity
    ids = jnp.sum(arrived_ref[:, capacity:, :].astype(jnp.float32), axis=0)
    lines = [ids[line : line + 1] for line in range(-(-slots // columns))]
    id_row = jnp.concatenate(lines, axis=1)[:, :slots]
    shape = (MAXP, doc_dev, slots)
    wanted = lax.broadcasted_iota(jnp.int32, shape, 0) + lax.broadcasted_iota(jnp.int32, shape, 1) * MAXP
    wanted = wanted.reshape(table_rows, slots).astype(jnp.float32) + 1.0
    chosen = jnp.where(wanted == id_row, 1.0, 0.0).astype(jnp.bfloat16)
    arrived = arrived_ref[:, :capacity, :].reshape(slots, columns)
    table = jnp.dot(chosen, arrived, preferred_element_type=jnp.float32)
    scores = table[:, :all_queries] + table[:, all_queries:]
    document = lax.broadcasted_iota(jnp.int32, (doc_dev, slots), 0).astype(jnp.float32)
    held = jnp.floor((id_row - 1.0) * (1.0 / MAXP)) == document
    count = jnp.sum(jnp.where(held, 1.0, 0.0), axis=1, keepdims=True)
    count = jnp.broadcast_to(count, (doc_dev, all_queries))
    scores = scores.reshape(MAXP, doc_dev, all_queries)
    places = [jnp.where(count > place, scores[place], very_negative) for place in range(MAXP)]
    highest = functools.reduce(jnp.maximum, places)
    total = functools.reduce(jnp.add, [jnp.exp(place - highest) for place in places])
    pooled = highest + jnp.log(total)
    active = notes_ref[2:3, :] > 0.0
    scores_ref[...] = jnp.where(active, pooled, 0.0)
    peak = jnp.max(highest, axis=0, keepdims=True)
    student = peak + jnp.log(jnp.sum(total * jnp.exp(highest - peak), axis=0, keepdims=True))
    student = jnp.where(active, student, very_negative)
    mean = notes_ref[1:2, :] - jnp.sum(weights_ref[...] * pooled, axis=0, keepdims=True)
    teacher = notes_ref[0:1, :]
    row = lax.broadcasted_iota(jnp.int32, lines_ref.shape, 0)
    lines = jnp.zeros(lines_ref.shape, jnp.float32)
    for block in range(query_groups):
        part = slice(block * rows_dev, (block + 1) * rows_dev)
        line = jnp.concatenate(
            [
                student[:, part],
                teacher[:, part],
                mean[:, part],
                jnp.zeros((1, lines_ref.shape[1] - 3 * rows_dev), jnp.float32),
            ],
            axis=1,
        )
        lines = jnp.where(row == block, jnp.broadcast_to(line, lines_ref.shape), lines)
    lines_ref[...] = lines


def order_kernel(rows_dev, query_groups, scores_ref, out_ref):
    out_ref[...] = from_first(scores_ref[...], lax.axis_index("qry"), rows_dev, query_groups)


def spread_kernel(first_place, *refs):
    line_refs, out_ref = refs[:-1], refs[-1]
    sources = len(line_refs)
    row = lax.broadcasted_iota(jnp.int32, out_ref.shape, 0)
    source = row % sources
    crossed = jnp.where(row // sources == first_place, 1, 0)
    here = jnp.where(lax.axis_index("doc") == 0, 1, 0)
    part = (crossed - here + sources) % sources
    out = jnp.zeros(out_ref.shape, jnp.float32)
    for k, lines in enumerate(line_refs):
        for ahead in range(sources):
            held = (ahead - k) % sources
            line = jnp.broadcast_to(lines[held : held + 1, :], out_ref.shape)
            out = jnp.where((source == k) & (part == ahead), line, out)
    out_ref[...] = out


def merge_kernel(rows_dev, parts_ref, out_ref):
    parts = parts_ref[...]
    peak = jnp.max(parts, axis=0, keepdims=True)
    weights = jnp.exp(parts - peak)
    total = jnp.sum(weights, axis=0, keepdims=True)
    moved = jnp.concatenate([weights[:, -rows_dev:], weights[:, :-rows_dev]], axis=1)
    weighted = jnp.sum(moved * parts, axis=0, keepdims=True)
    totals = peak + jnp.log(total)
    columns = [slice(k * rows_dev, (k + 1) * rows_dev) for k in range(3)]
    out_ref[...] = (
        weighted[:, columns[2]] / total[:, columns[1]] - totals[:, columns[1]] + totals[:, columns[0]]
    )


def call(kernel, out_shape, in_specs, scratch=(), **cost):
    several = isinstance(out_shape, (list, tuple))
    return pl.pallas_call(
        kernel,
        out_shape=out_shape,
        in_specs=in_specs,
        out_specs=[VMEM] * len(out_shape) if several else VMEM,
        scratch_shapes=scratch,
        compiler_params=pltpu.CompilerParams(vmem_limit_bytes=16 * 1024 * 1024),
        cost_estimate=pl.CostEstimate(**cost) if cost else None,
    )


def crossed_groups(order, query_groups):
    return [
        [doc * query_groups + (core + (doc == 0)) % query_groups for doc in order]
        for core in range(query_groups)
    ]


def shuffled_from(first, size):
    others = [k for k in range(size) if k != first]
    return [first] + random.Random(ORDER_SEED).sample(others, size - 1)


def from_others(array, query_groups):
    return [
        lax.ppermute(array, "qry", [((i + k) % query_groups, i) for i in range(query_groups)])
        for k in range(1, query_groups)
    ]


def on_device(queries, passages, passage_route, pattern, teacher):
    doc_count = lax.axis_size("doc")
    query_groups = lax.axis_size("qry")
    devices = doc_count * query_groups
    rows_dev, width = queries.shape
    rows = passages.shape[0]
    all_queries, doc_dev = teacher.shape
    table_rows = doc_dev * MAXP
    capacity = -(-table_rows // (doc_count * PACKED)) * PACKED
    last_doc = doc_count - 1
    order = shuffled_from(last_doc, doc_count)
    route_order = shuffled_from(last_doc - doc_count // 4, doc_count)
    f32, bf16 = jnp.float32, jnp.bfloat16
    shaped = jax.ShapeDtypeStruct

    others = from_others(queries, query_groups)
    held, own, place, ids, weights, notes = call(
        functools.partial(
            before_kernel,
            (doc_count, query_groups, capacity, table_rows, rows_dev, route_order),
        ),
        [
            shaped((rows, width), bf16),
            shaped((rows_dev, width), bf16),
            shaped((doc_count * capacity, rows), bf16),
            shaped((doc_count * SUBLANES, 2 * all_queries), f32),
            shaped((doc_dev, all_queries), f32),
            shaped((SUBLANES, all_queries), f32),
        ],
        [HBM] * 5,
        [
            pltpu.VMEM((1, rows), jnp.int32),
            pltpu.VMEM(pattern.shape, jnp.int32),
            pltpu.VMEM((doc_dev, all_queries), f32),
            pltpu.SemaphoreType.DMA(()),
            pltpu.SemaphoreType.DMA((4,)),
        ],
        flops=doc_count * capacity * rows,
        bytes_accessed=2 * (rows + rows_dev) * width,
        transcendentals=0,
    )(
        *[
            pltpu.with_memory_space_constraint(array, pltpu.HBM)
            for array in (passages, queries, passage_route.reshape(1, rows), pattern, teacher.T)
        ]
    )
    outgoing = call(
        pack_kernel,
        shaped((doc_count, capacity + SUBLANES, 2 * all_queries), bf16),
        [VMEM] * (4 + len(others)),
    )(held, place, ids, own, *others)
    arrived = lax.all_to_all(
        outgoing,
        "doc",
        split_axis=0,
        concat_axis=0,
        axis_index_groups=[route_order],
        tiled=True,
    )
    line = -(-3 * rows_dev // LANES) * LANES
    lines_rows = -(-query_groups // SUBLANES) * SUBLANES
    doc_scores, lines = call(
        functools.partial(pool_kernel, rows_dev, query_groups),
        [shaped((doc_dev, all_queries), f32), shaped((lines_rows, line), f32)],
        [VMEM, VMEM, VMEM],
    )(arrived, weights, notes)
    received = from_others(lines, query_groups)
    doc_scores = call(
        functools.partial(order_kernel, rows_dev, query_groups),
        shaped((doc_dev, all_queries), f32),
        [VMEM],
    )(doc_scores)
    doc_scores, received = lax.optimization_barrier((doc_scores, received))
    partials = call(
        functools.partial(spread_kernel, order.index(0)),
        shaped((devices, line), f32),
        [VMEM] * query_groups,
    )(lines, *received)
    everyone = lax.all_to_all(
        partials,
        ("doc", "qry"),
        split_axis=0,
        concat_axis=0,
        axis_index_groups=crossed_groups(order, query_groups),
        tiled=True,
    )
    divergence = call(
        functools.partial(merge_kernel, rows_dev), shaped((1, rows_dev), f32), [VMEM]
    )(everyone)
    return (doc_scores.T, divergence.reshape(rows_dev))


def solution(mesh):
    in_specs = (
        P("qry", None),
        P(("doc", "qry"), None),
        P(("doc", "qry")),
        P(),
        P(None, ("doc", "qry")),
    )
    out_specs = (P(None, ("doc", "qry")), P("qry"))
    return jax.shard_map(
        on_device, mesh=mesh, in_specs=in_specs, out_specs=out_specs, check_vma=False
    )
```

```python
import functools
import random

import jax
import jax.numpy as jnp
from jax import lax
from jax.experimental import pallas as pl
from jax.experimental.pallas import tpu as pltpu
from jax.sharding import PartitionSpec as P

MAXP = 16
LANES = 128
SUBLANES = 8
PACKED = 16
ORDER_SEED = 25

score_scale = 0.03125
very_negative = -1e30

VMEM = pl.BlockSpec(memory_space=pltpu.VMEM)
HBM = pl.BlockSpec(memory_space=pltpu.HBM)
NT = (((1,), (1,)), ((), ()))


def place_in(order, index):
    out = jnp.zeros(index.shape, jnp.int32)
    for place, entry in enumerate(order):
        out = jnp.where(index == entry, place, out)
    return out


def rolled(array, columns):
    if columns == 0:
        return array
    return jnp.concatenate([array[:, columns:], array[:, :columns]], axis=1)


def from_own(array, core, rows_dev, query_groups):
    out = array
    for mine in range(1, query_groups):
        out = jnp.where(core == mine, rolled(array, mine * rows_dev), out)
    return out


def from_first(array, core, rows_dev, query_groups):
    out = array
    for mine in range(1, query_groups):
        out = jnp.where(core == mine, rolled(array, (query_groups - mine) * rows_dev), out)
    return out


def dot_nt(a, b):
    return lax.dot_general(a, b, NT, preferred_element_type=jnp.float32)


def before_kernel(
    sizes, passages_hbm, own_hbm, route_hbm, pattern_hbm, teacher_hbm,
    passages_ref, own_ref, place_ref, ids_ref, weights_ref, notes_ref,
    route_ref, pattern_ref, teacher_ref, passages_sem, small_sem,
):
    doc_count, query_groups, capacity, table_rows, rows_dev, order = sizes
    rows = passages_ref.shape[0]
    pairs = [
        (route_hbm, route_ref),
        (pattern_hbm, pattern_ref),
        (teacher_hbm, teacher_ref),
        (own_hbm, own_ref),
    ]
    small = [
        pltpu.make_async_copy(source, target, small_sem.at[k])
        for k, (source, target) in enumerate(pairs)
    ]
    large = pltpu.make_async_copy(passages_hbm, passages_ref, passages_sem)
    small[0].start()
    large.start()
    for copy in small[1:]:
        copy.start()
    core = lax.axis_index("qry")
    group_id = lax.axis_index("doc") * query_groups + core

    small[0].wait()
    route = route_ref[...]
    owner = route // table_rows
    target = place_in(order, owner // query_groups).astype(jnp.float32)
    slot = (route - owner * table_rows).astype(jnp.float32)
    down = lax.broadcasted_iota(jnp.int32, (rows, rows), 0)
    across = lax.broadcasted_iota(jnp.int32, (rows, rows), 1)

    def as_column(row):
        row = jnp.broadcast_to(row, (rows, rows))
        return jnp.sum(jnp.where(down == across, row, 0.0), axis=1, keepdims=True)

    earlier = (as_column(target) == target) & (down < across)
    position = jnp.sum(jnp.where(earlier, 1.0, 0.0), axis=0, keepdims=True)
    placing = target * capacity + position
    outgoing = lax.broadcasted_iota(jnp.int32, (doc_count * capacity, rows), 0).astype(jnp.float32)
    place_ref[...] = jnp.where(outgoing == placing, 1.0, 0.0).astype(place_ref.dtype)
    columns = ids_ref.shape[1]
    mine = place_in(order, jnp.full((1, 1), lax.axis_index("doc"), jnp.int32)) * capacity
    arriving = as_column(position) + mine.astype(jnp.float32)
    number = as_column(slot) + 1.0
    row = lax.broadcasted_iota(jnp.int32, (ids_ref.shape[0], rows), 0)
    column = lax.broadcasted_iota(jnp.int32, (rows, columns), 1).astype(jnp.float32)
    ids = jnp.zeros(ids_ref.shape, jnp.float32)
    for line in range(-(-doc_count * capacity // columns)):
        goes = ((row // SUBLANES).astype(jnp.float32) == target) & (row % SUBLANES == line)
        goes = jnp.where(goes, 1.0, 0.0).astype(jnp.bfloat16)
        here = jnp.where(column + float(line * columns) == arriving, number, 0.0)
        ids += jnp.dot(goes, here.astype(jnp.bfloat16), preferred_element_type=jnp.float32)
    ids_ref[...] = ids

    small[1].wait()
    small[2].wait()
    all_queries = rows_dev * query_groups
    lane = lax.broadcasted_iota(jnp.int32, (1, all_queries), 1)
    own = lax.broadcasted_iota(jnp.int32, pattern_ref.shape, 1) == group_id
    flags = jnp.sum(jnp.where(own, pattern_ref[...], 0), axis=1, keepdims=True)
    active = jnp.zeros((1, all_queries), jnp.float32)
    for block in range(query_groups):
        inside = (lane >= block * rows_dev) & (lane < (block + 1) * rows_dev)
        flag = jnp.broadcast_to(flags[block : block + 1], (1, all_queries))
        active = jnp.where(inside & (flag > 0), 1.0, active)
    active = from_own(active, core, rows_dev, query_groups)
    teacher = from_own(teacher_ref[...], core, rows_dev, query_groups)
    peak = jnp.max(teacher, axis=0, keepdims=True)
    weights = jnp.exp(teacher - peak)
    weight_sum = jnp.sum(weights, axis=0, keepdims=True)
    weights = weights / weight_sum
    weights_ref[...] = weights
    notes_ref[0:1, :] = jnp.where(active > 0.0, peak + jnp.log(weight_sum), very_negative)
    notes_ref[1:2, :] = jnp.sum(weights * teacher, axis=0, keepdims=True)
    notes_ref[2:3, :] = active
    notes_ref[3:, :] = jnp.zeros((notes_ref.shape[0] - 3, all_queries), jnp.float32)
    small[3].wait()
    large.wait()


def pack_kernel(passages_ref, place_ref, ids_ref, *refs):
    query_refs, out_ref = refs[:-1], refs[-1]
    doc_count, block_rows, columns = out_ref.shape
    capacity = block_rows - SUBLANES
    queries = jnp.concatenate([part[...] for part in query_refs], axis=0)
    logits = dot_nt(passages_ref[...], queries) * score_scale
    high = logits.astype(jnp.bfloat16)
    low = (logits - high.astype(jnp.float32)).astype(jnp.bfloat16)
    placed = jnp.dot(
        place_ref[...], jnp.concatenate([high, low], axis=1), preferred_element_type=jnp.float32
    )
    out_ref[:, :capacity, :] = placed.reshape(doc_count, capacity, columns).astype(out_ref.dtype)
    ids = ids_ref[...].reshape(doc_count, SUBLANES, columns)
    out_ref[:, capacity:, :] = ids.astype(out_ref.dtype)


def pool_kernel(rows_dev, query_groups, arrived_ref, weights_ref, notes_ref, scores_ref, lines_ref):
    doc_dev, all_queries = weights_ref.shape
    table_rows = doc_dev * MAXP
    doc_count, block_rows, columns = arrived_ref.shape
    capacity = block_rows - SUBLANES
    slots = doc_count * capacity
    ids = jnp.sum(arrived_ref[:, capacity:, :].astype(jnp.float32), axis=0)
    lines = [ids[line : line + 1] for line in range(-(-slots // columns))]
    id_row = jnp.concatenate(lines, axis=1)[:, :slots]
    shape = (MAXP, doc_dev, slots)
    wanted = lax.broadcasted_iota(jnp.int32, shape, 0) + lax.broadcasted_iota(jnp.int32, shape, 1) * MAXP
    wanted = wanted.reshape(table_rows, slots).astype(jnp.float32) + 1.0
    chosen = jnp.where(wanted == id_row, 1.0, 0.0).astype(jnp.bfloat16)
    arrived = arrived_ref[:, :capacity, :].reshape(slots, columns)
    table = jnp.dot(chosen, arrived, preferred_element_type=jnp.float32)
    scores = table[:, :all_queries] + table[:, all_queries:]
    document = lax.broadcasted_iota(jnp.int32, (doc_dev, slots), 0).astype(jnp.float32)
    held = jnp.floor((id_row - 1.0) * (1.0 / MAXP)) == document
    count = jnp.sum(jnp.where(held, 1.0, 0.0), axis=1, keepdims=True)
    count = jnp.broadcast_to(count, (doc_dev, all_queries))
    scores = scores.reshape(MAXP, doc_dev, all_queries)
    places = [jnp.where(count > place, scores[place], very_negative) for place in range(MAXP)]
    highest = functools.reduce(jnp.maximum, places)
    total = functools.reduce(jnp.add, [jnp.exp(place - highest) for place in places])
    pooled = highest + jnp.log(total)
    active = notes_ref[2:3, :] > 0.0
    scores_ref[...] = jnp.where(active, pooled, 0.0)
    peak = jnp.max(highest, axis=0, keepdims=True)
    student = peak + jnp.log(jnp.sum(total * jnp.exp(highest - peak), axis=0, keepdims=True))
    student = jnp.where(active, student, very_negative)
    mean = notes_ref[1:2, :] - jnp.sum(weights_ref[...] * pooled, axis=0, keepdims=True)
    teacher = notes_ref[0:1, :]
    row = lax.broadcasted_iota(jnp.int32, lines_ref.shape, 0)
    lines = jnp.zeros(lines_ref.shape, jnp.float32)
    for block in range(query_groups):
        part = slice(block * rows_dev, (block + 1) * rows_dev)
        line = jnp.concatenate(
            [
                student[:, part],
                teacher[:, part],
                mean[:, part],
                jnp.zeros((1, lines_ref.shape[1] - 3 * rows_dev), jnp.float32),
            ],
            axis=1,
        )
        lines = jnp.where(row == block, jnp.broadcast_to(line, lines_ref.shape), lines)
    lines_ref[...] = lines


def order_kernel(rows_dev, query_groups, scores_ref, out_ref):
    out_ref[...] = from_first(scores_ref[...], lax.axis_index("qry"), rows_dev, query_groups)


def joined(parts, rows_dev):
    peak = functools.reduce(jnp.maximum, parts)
    weights = [jnp.exp(part - peak) for part in parts]
    total = functools.reduce(jnp.add, weights)
    moved = [rolled(weight, weight.shape[1] - rows_dev) for weight in weights + [total]]
    weighted = functools.reduce(jnp.add, [w * part for w, part in zip(moved, parts)])
    lane = lax.broadcasted_iota(jnp.int32, peak.shape, 1)
    totals = peak + jnp.log(total)
    return jnp.where(lane < 2 * rows_dev, totals, weighted / moved[-1])


def spread_kernel(first_place, rows_dev, *refs):
    line_refs, out_ref = refs[:-1], refs[-1]
    sources = len(line_refs)
    place = lax.broadcasted_iota(jnp.int32, out_ref.shape, 0)
    crossed = jnp.where(place == first_place, 1, 0)
    here = jnp.where(lax.axis_index("doc") == 0, 1, 0)
    part = (crossed - here + sources) % sources
    out = jnp.zeros(out_ref.shape, jnp.float32)
    for ahead in range(sources):
        held = [(ahead - k) % sources for k in range(sources)]
        line = joined([lines[h : h + 1, :] for lines, h in zip(line_refs, held)], rows_dev)
        out = jnp.where(part == ahead, jnp.broadcast_to(line, out_ref.shape), out)
    out_ref[...] = out


def merge_kernel(rows_dev, parts_ref, out_ref):
    parts = parts_ref[...]
    peak = jnp.max(parts, axis=0, keepdims=True)
    weights = jnp.exp(parts - peak)
    total = jnp.sum(weights, axis=0, keepdims=True)
    moved = jnp.concatenate([weights[:, -rows_dev:], weights[:, :-rows_dev]], axis=1)
    weighted = jnp.sum(moved * parts, axis=0, keepdims=True)
    totals = peak + jnp.log(total)
    columns = [slice(k * rows_dev, (k + 1) * rows_dev) for k in range(3)]
    out_ref[...] = (
        weighted[:, columns[2]] / total[:, columns[1]] - totals[:, columns[1]] + totals[:, columns[0]]
    )


def call(kernel, out_shape, in_specs, scratch=(), **cost):
    several = isinstance(out_shape, (list, tuple))
    return pl.pallas_call(
        kernel,
        out_shape=out_shape,
        in_specs=in_specs,
        out_specs=[VMEM] * len(out_shape) if several else VMEM,
        scratch_shapes=scratch,
        compiler_params=pltpu.CompilerParams(vmem_limit_bytes=16 * 1024 * 1024),
        cost_estimate=pl.CostEstimate(**cost) if cost else None,
    )


def crossed_groups(order, query_groups):
    return [
        [doc * query_groups + (core + (doc == 0)) % query_groups for doc in order]
        for core in range(query_groups)
    ]


def shuffled_from(first, size):
    others = [k for k in range(size) if k != first]
    return [first] + random.Random(ORDER_SEED).sample(others, size - 1)


def from_others(array, query_groups):
    return [
        lax.ppermute(array, "qry", [((i + k) % query_groups, i) for i in range(query_groups)])
        for k in range(1, query_groups)
    ]


def on_device(queries, passages, passage_route, pattern, teacher):
    doc_count = lax.axis_size("doc")
    query_groups = lax.axis_size("qry")
    rows_dev, width = queries.shape
    rows = passages.shape[0]
    all_queries, doc_dev = teacher.shape
    table_rows = doc_dev * MAXP
    capacity = -(-table_rows // (doc_count * PACKED)) * PACKED
    last_doc = doc_count - 1
    order = shuffled_from(last_doc, doc_count)
    route_order = shuffled_from(last_doc - doc_count // 4, doc_count)
    f32, bf16 = jnp.float32, jnp.bfloat16
    shaped = jax.ShapeDtypeStruct

    others = from_others(queries, query_groups)
    held, own, place, ids, weights, notes = call(
        functools.partial(
            before_kernel,
            (doc_count, query_groups, capacity, table_rows, rows_dev, route_order),
        ),
        [
            shaped((rows, width), bf16),
            shaped((rows_dev, width), bf16),
            shaped((doc_count * capacity, rows), bf16),
            shaped((doc_count * SUBLANES, 2 * all_queries), f32),
            shaped((doc_dev, all_queries), f32),
            shaped((SUBLANES, all_queries), f32),
        ],
        [HBM] * 5,
        [
            pltpu.VMEM((1, rows), jnp.int32),
            pltpu.VMEM(pattern.shape, jnp.int32),
            pltpu.VMEM((doc_dev, all_queries), f32),
            pltpu.SemaphoreType.DMA(()),
            pltpu.SemaphoreType.DMA((4,)),
        ],
        flops=doc_count * capacity * rows,
        bytes_accessed=2 * (rows + rows_dev) * width,
        transcendentals=0,
    )(
        *[
            pltpu.with_memory_space_constraint(array, pltpu.HBM)
            for array in (passages, queries, passage_route.reshape(1, rows), pattern, teacher.T)
        ]
    )
    outgoing = call(
        pack_kernel,
        shaped((doc_count, capacity + SUBLANES, 2 * all_queries), bf16),
        [VMEM] * (4 + len(others)),
    )(held, place, ids, own, *others)
    arrived = lax.all_to_all(
        outgoing,
        "doc",
        split_axis=0,
        concat_axis=0,
        axis_index_groups=[route_order],
        tiled=True,
    )
    line = -(-3 * rows_dev // LANES) * LANES
    lines_rows = -(-query_groups // SUBLANES) * SUBLANES
    doc_scores, lines = call(
        functools.partial(pool_kernel, rows_dev, query_groups),
        [shaped((doc_dev, all_queries), f32), shaped((lines_rows, line), f32)],
        [VMEM, VMEM, VMEM],
    )(arrived, weights, notes)
    received = from_others(lines, query_groups)
    doc_scores = call(
        functools.partial(order_kernel, rows_dev, query_groups),
        shaped((doc_dev, all_queries), f32),
        [VMEM],
    )(doc_scores)
    doc_scores, received = lax.optimization_barrier((doc_scores, received))
    partials = call(
        functools.partial(spread_kernel, order.index(0), rows_dev),
        shaped((doc_count, line), f32),
        [VMEM] * query_groups,
    )(lines, *received)
    everyone = lax.all_to_all(
        partials,
        ("doc", "qry"),
        split_axis=0,
        concat_axis=0,
        axis_index_groups=crossed_groups(order, query_groups),
        tiled=True,
    )
    divergence = call(
        functools.partial(merge_kernel, rows_dev), shaped((1, rows_dev), f32), [VMEM]
    )(everyone)
    return (doc_scores.T, divergence.reshape(rows_dev))


def solution(mesh):
    in_specs = (
        P("qry", None),
        P(("doc", "qry"), None),
        P(("doc", "qry")),
        P(),
        P(None, ("doc", "qry")),
    )
    out_specs = (P(None, ("doc", "qry")), P("qry"))
    return jax.shard_map(
        on_device, mesh=mesh, in_specs=in_specs, out_specs=out_specs, check_vma=False
    )
```

```python
import functools
import random

import jax
import jax.numpy as jnp
from jax import lax
from jax.experimental import pallas as pl
from jax.experimental.pallas import tpu as pltpu
from jax.sharding import PartitionSpec as P

MAXP = 16
LANES = 128
SUBLANES = 8
PACKED = 16
ORDER_SEED = 25

score_scale = 0.03125
very_negative = -1e30

VMEM = pl.BlockSpec(memory_space=pltpu.VMEM)
HBM = pl.BlockSpec(memory_space=pltpu.HBM)
NT = (((1,), (1,)), ((), ()))


def place_in(order, index):
    out = jnp.zeros(index.shape, jnp.int32)
    for place, entry in enumerate(order):
        out = jnp.where(index == entry, place, out)
    return out


def rolled(array, columns):
    if columns == 0:
        return array
    return jnp.concatenate([array[:, columns:], array[:, :columns]], axis=1)


def from_own(array, core, rows_dev, query_groups):
    out = array
    for mine in range(1, query_groups):
        out = jnp.where(core == mine, rolled(array, mine * rows_dev), out)
    return out


def from_first(array, core, rows_dev, query_groups):
    out = array
    for mine in range(1, query_groups):
        out = jnp.where(core == mine, rolled(array, (query_groups - mine) * rows_dev), out)
    return out


def dot_nt(a, b):
    return lax.dot_general(a, b, NT, preferred_element_type=jnp.float32)


def before_kernel(
    sizes, passages_hbm, own_hbm, route_hbm, pattern_hbm, teacher_hbm,
    passages_ref, own_ref, place_ref, ids_ref, weights_ref, notes_ref,
    route_ref, pattern_ref, teacher_ref, passages_sem, small_sem,
):
    doc_count, query_groups, capacity, table_rows, rows_dev, order = sizes
    rows = passages_ref.shape[0]
    pairs = [
        (route_hbm, route_ref),
        (pattern_hbm, pattern_ref),
        (teacher_hbm, teacher_ref),
        (own_hbm, own_ref),
    ]
    small = [
        pltpu.make_async_copy(source, target, small_sem.at[k])
        for k, (source, target) in enumerate(pairs)
    ]
    large = pltpu.make_async_copy(passages_hbm, passages_ref, passages_sem)
    small[0].start()
    large.start()
    for copy in small[1:]:
        copy.start()
    core = lax.axis_index("qry")
    group_id = lax.axis_index("doc") * query_groups + core

    small[0].wait()
    route = route_ref[...]
    owner = route // table_rows
    target = place_in(order, owner // query_groups).astype(jnp.float32)
    slot = (route - owner * table_rows).astype(jnp.float32)
    down = lax.broadcasted_iota(jnp.int32, (rows, rows), 0)
    across = lax.broadcasted_iota(jnp.int32, (rows, rows), 1)

    def as_column(row):
        row = jnp.broadcast_to(row, (rows, rows))
        return jnp.sum(jnp.where(down == across, row, 0.0), axis=1, keepdims=True)

    earlier = (as_column(target) == target) & (down < across)
    position = jnp.sum(jnp.where(earlier, 1.0, 0.0), axis=0, keepdims=True)
    placing = target * capacity + position
    outgoing = lax.broadcasted_iota(jnp.int32, (doc_count * capacity, rows), 0).astype(jnp.float32)
    place_ref[...] = jnp.where(outgoing == placing, score_scale, 0.0).astype(place_ref.dtype)
    columns = ids_ref.shape[1]
    mine = place_in(order, jnp.full((1, 1), lax.axis_index("doc"), jnp.int32)) * capacity
    arriving = as_column(position) + mine.astype(jnp.float32)
    number = as_column(slot) + 1.0
    row = lax.broadcasted_iota(jnp.int32, (ids_ref.shape[0], rows), 0)
    column = lax.broadcasted_iota(jnp.int32, (rows, columns), 1).astype(jnp.float32)
    ids = jnp.zeros(ids_ref.shape, jnp.float32)
    for line in range(-(-doc_count * capacity // columns)):
        goes = ((row // SUBLANES).astype(jnp.float32) == target) & (row % SUBLANES == line)
        goes = jnp.where(goes, 1.0, 0.0).astype(jnp.bfloat16)
        here = jnp.where(column + float(line * columns) == arriving, number, 0.0)
        ids += jnp.dot(goes, here.astype(jnp.bfloat16), preferred_element_type=jnp.float32)
    ids_ref[...] = ids

    small[1].wait()
    small[2].wait()
    all_queries = rows_dev * query_groups
    lane = lax.broadcasted_iota(jnp.int32, (1, all_queries), 1)
    own = lax.broadcasted_iota(jnp.int32, pattern_ref.shape, 1) == group_id
    flags = jnp.sum(jnp.where(own, pattern_ref[...], 0), axis=1, keepdims=True)
    active = jnp.zeros((1, all_queries), jnp.float32)
    for block in range(query_groups):
        inside = (lane >= block * rows_dev) & (lane < (block + 1) * rows_dev)
        flag = jnp.broadcast_to(flags[block : block + 1], (1, all_queries))
        active = jnp.where(inside & (flag > 0), 1.0, active)
    active = from_own(active, core, rows_dev, query_groups)
    teacher = from_own(teacher_ref[...], core, rows_dev, query_groups)
    peak = jnp.max(teacher, axis=0, keepdims=True)
    weights = jnp.exp(teacher - peak)
    weight_sum = jnp.sum(weights, axis=0, keepdims=True)
    weights = weights / weight_sum
    weights_ref[...] = weights
    notes_ref[0:1, :] = jnp.where(active > 0.0, peak + jnp.log(weight_sum), very_negative)
    notes_ref[1:2, :] = jnp.sum(weights * teacher, axis=0, keepdims=True)
    notes_ref[2:3, :] = active
    notes_ref[3:, :] = jnp.zeros((notes_ref.shape[0] - 3, all_queries), jnp.float32)
    small[3].wait()
    large.wait()


def pack_kernel(passages_ref, place_ref, ids_ref, *refs):
    query_refs, out_ref = refs[:-1], refs[-1]
    doc_count, block_rows, columns = out_ref.shape
    capacity = block_rows - SUBLANES
    queries = jnp.concatenate([part[...] for part in query_refs], axis=0)
    logits = dot_nt(passages_ref[...], queries)
    high = logits.astype(jnp.bfloat16)
    low = (logits - high.astype(jnp.float32)).astype(jnp.bfloat16)
    placed = jnp.dot(
        place_ref[...], jnp.concatenate([high, low], axis=1), preferred_element_type=jnp.float32
    )
    out_ref[:, :capacity, :] = placed.reshape(doc_count, capacity, columns).astype(out_ref.dtype)
    ids = ids_ref[...].reshape(doc_count, SUBLANES, columns)
    out_ref[:, capacity:, :] = ids.astype(out_ref.dtype)


def pool_kernel(rows_dev, query_groups, arrived_ref, weights_ref, notes_ref, scores_ref, lines_ref):
    doc_dev, all_queries = weights_ref.shape
    table_rows = doc_dev * MAXP
    doc_count, block_rows, columns = arrived_ref.shape
    capacity = block_rows - SUBLANES
    slots = doc_count * capacity
    ids = jnp.sum(arrived_ref[:, capacity:, :].astype(jnp.float32), axis=0)
    lines = [ids[line : line + 1] for line in range(-(-slots // columns))]
    id_row = jnp.concatenate(lines, axis=1)[:, :slots]
    shape = (MAXP, doc_dev, slots)
    wanted = lax.broadcasted_iota(jnp.int32, shape, 0) + lax.broadcasted_iota(jnp.int32, shape, 1) * MAXP
    wanted = wanted.reshape(table_rows, slots).astype(jnp.float32) + 1.0
    chosen = jnp.where(wanted == id_row, 1.0, 0.0).astype(jnp.bfloat16)
    arrived = arrived_ref[:, :capacity, :].reshape(slots, columns)
    table = jnp.dot(chosen, arrived, preferred_element_type=jnp.float32)
    scores = table[:, :all_queries] + table[:, all_queries:]
    document = lax.broadcasted_iota(jnp.int32, (doc_dev, slots), 0).astype(jnp.float32)
    held = jnp.floor((id_row - 1.0) * (1.0 / MAXP)) == document
    count = jnp.sum(jnp.where(held, 1.0, 0.0), axis=1, keepdims=True)
    count = jnp.broadcast_to(count, (doc_dev, all_queries))
    scores = scores.reshape(MAXP, doc_dev, all_queries)
    places = [jnp.where(count > place, scores[place], very_negative) for place in range(MAXP)]
    highest = functools.reduce(jnp.maximum, places)
    total = functools.reduce(jnp.add, [jnp.exp(place - highest) for place in places])
    pooled = highest + jnp.log(total)
    active = notes_ref[2:3, :] > 0.0
    scores_ref[...] = jnp.where(active, pooled, 0.0)
    peak = jnp.max(highest, axis=0, keepdims=True)
    student = peak + jnp.log(jnp.sum(total * jnp.exp(highest - peak), axis=0, keepdims=True))
    student = jnp.where(active, student, very_negative)
    mean = notes_ref[1:2, :] - jnp.sum(weights_ref[...] * pooled, axis=0, keepdims=True)
    teacher = notes_ref[0:1, :]
    row = lax.broadcasted_iota(jnp.int32, lines_ref.shape, 0)
    lines = jnp.zeros(lines_ref.shape, jnp.float32)
    for block in range(query_groups):
        part = slice(block * rows_dev, (block + 1) * rows_dev)
        line = jnp.concatenate(
            [
                student[:, part],
                teacher[:, part],
                mean[:, part],
                jnp.zeros((1, lines_ref.shape[1] - 3 * rows_dev), jnp.float32),
            ],
            axis=1,
        )
        lines = jnp.where(row == block, jnp.broadcast_to(line, lines_ref.shape), lines)
    lines_ref[...] = lines


def order_kernel(rows_dev, query_groups, scores_ref, out_ref):
    out_ref[...] = from_first(scores_ref[...], lax.axis_index("qry"), rows_dev, query_groups)


def joined(parts, rows_dev):
    peak = functools.reduce(jnp.maximum, parts)
    weights = [jnp.exp(part - peak) for part in parts]
    total = functools.reduce(jnp.add, weights)
    moved = [rolled(weight, weight.shape[1] - rows_dev) for weight in weights + [total]]
    weighted = functools.reduce(jnp.add, [w * part for w, part in zip(moved, parts)])
    lane = lax.broadcasted_iota(jnp.int32, peak.shape, 1)
    totals = peak + jnp.log(total)
    return jnp.where(lane < 2 * rows_dev, totals, weighted / moved[-1])


def spread_kernel(first_place, rows_dev, *refs):
    line_refs, out_ref = refs[:-1], refs[-1]
    sources = len(line_refs)
    place = lax.broadcasted_iota(jnp.int32, out_ref.shape, 0)
    crossed = jnp.where(place == first_place, 1, 0)
    here = jnp.where(lax.axis_index("doc") == 0, 1, 0)
    part = (crossed - here + sources) % sources
    out = jnp.zeros(out_ref.shape, jnp.float32)
    for ahead in range(sources):
        held = [(ahead - k) % sources for k in range(sources)]
        line = joined([lines[h : h + 1, :] for lines, h in zip(line_refs, held)], rows_dev)
        out = jnp.where(part == ahead, jnp.broadcast_to(line, out_ref.shape), out)
    out_ref[...] = out


def merge_kernel(rows_dev, parts_ref, out_ref):
    parts = parts_ref[...]
    peak = jnp.max(parts, axis=0, keepdims=True)
    weights = jnp.exp(parts - peak)
    total = jnp.sum(weights, axis=0, keepdims=True)
    moved = jnp.concatenate([weights[:, -rows_dev:], weights[:, :-rows_dev]], axis=1)
    weighted = jnp.sum(moved * parts, axis=0, keepdims=True)
    totals = peak + jnp.log(total)
    columns = [slice(k * rows_dev, (k + 1) * rows_dev) for k in range(3)]
    out_ref[...] = (
        weighted[:, columns[2]] / total[:, columns[1]] - totals[:, columns[1]] + totals[:, columns[0]]
    )


def call(kernel, out_shape, in_specs, scratch=(), **cost):
    several = isinstance(out_shape, (list, tuple))
    return pl.pallas_call(
        kernel,
        out_shape=out_shape,
        in_specs=in_specs,
        out_specs=[VMEM] * len(out_shape) if several else VMEM,
        scratch_shapes=scratch,
        compiler_params=pltpu.CompilerParams(vmem_limit_bytes=16 * 1024 * 1024),
        cost_estimate=pl.CostEstimate(**cost) if cost else None,
    )


def crossed_groups(order, query_groups):
    return [
        [doc * query_groups + (core + (doc == 0)) % query_groups for doc in order]
        for core in range(query_groups)
    ]


def shuffled_from(first, size):
    others = [k for k in range(size) if k != first]
    return [first] + random.Random(ORDER_SEED).sample(others, size - 1)


def from_others(array, query_groups):
    return [
        lax.ppermute(array, "qry", [((i + k) % query_groups, i) for i in range(query_groups)])
        for k in range(1, query_groups)
    ]


def on_device(queries, passages, passage_route, pattern, teacher):
    doc_count = lax.axis_size("doc")
    query_groups = lax.axis_size("qry")
    rows_dev, width = queries.shape
    rows = passages.shape[0]
    all_queries, doc_dev = teacher.shape
    table_rows = doc_dev * MAXP
    capacity = -(-table_rows // (doc_count * PACKED)) * PACKED
    last_doc = doc_count - 1
    order = shuffled_from(last_doc, doc_count)
    route_order = shuffled_from(last_doc - doc_count // 4, doc_count)
    f32, bf16 = jnp.float32, jnp.bfloat16
    shaped = jax.ShapeDtypeStruct

    others = from_others(queries, query_groups)
    held, own, place, ids, weights, notes = call(
        functools.partial(
            before_kernel,
            (doc_count, query_groups, capacity, table_rows, rows_dev, route_order),
        ),
        [
            shaped((rows, width), bf16),
            shaped((rows_dev, width), bf16),
            shaped((doc_count * capacity, rows), bf16),
            shaped((doc_count * SUBLANES, 2 * all_queries), f32),
            shaped((doc_dev, all_queries), f32),
            shaped((SUBLANES, all_queries), f32),
        ],
        [HBM] * 5,
        [
            pltpu.VMEM((1, rows), jnp.int32),
            pltpu.VMEM(pattern.shape, jnp.int32),
            pltpu.VMEM((doc_dev, all_queries), f32),
            pltpu.SemaphoreType.DMA(()),
            pltpu.SemaphoreType.DMA((4,)),
        ],
        flops=doc_count * capacity * rows,
        bytes_accessed=2 * (rows + rows_dev) * width,
        transcendentals=0,
    )(
        *[
            pltpu.with_memory_space_constraint(array, pltpu.HBM)
            for array in (passages, queries, passage_route.reshape(1, rows), pattern, teacher.T)
        ]
    )
    outgoing = call(
        pack_kernel,
        shaped((doc_count, capacity + SUBLANES, 2 * all_queries), bf16),
        [VMEM] * (4 + len(others)),
    )(held, place, ids, own, *others)
    arrived = lax.all_to_all(
        outgoing,
        "doc",
        split_axis=0,
        concat_axis=0,
        axis_index_groups=[route_order],
        tiled=True,
    )
    line = -(-3 * rows_dev // LANES) * LANES
    lines_rows = -(-query_groups // SUBLANES) * SUBLANES
    doc_scores, lines = call(
        functools.partial(pool_kernel, rows_dev, query_groups),
        [shaped((doc_dev, all_queries), f32), shaped((lines_rows, line), f32)],
        [VMEM, VMEM, VMEM],
    )(arrived, weights, notes)
    received = from_others(lines, query_groups)
    doc_scores = call(
        functools.partial(order_kernel, rows_dev, query_groups),
        shaped((doc_dev, all_queries), f32),
        [VMEM],
    )(doc_scores)
    doc_scores, received = lax.optimization_barrier((doc_scores, received))
    partials = call(
        functools.partial(spread_kernel, order.index(0), rows_dev),
        shaped((doc_count, line), f32),
        [VMEM] * query_groups,
    )(lines, *received)
    everyone = lax.all_to_all(
        partials,
        ("doc", "qry"),
        split_axis=0,
        concat_axis=0,
        axis_index_groups=crossed_groups(order, query_groups),
        tiled=True,
    )
    divergence = call(
        functools.partial(merge_kernel, rows_dev), shaped((1, rows_dev), f32), [VMEM]
    )(everyone)
    return (doc_scores.T, divergence.reshape(rows_dev))


def solution(mesh):
    in_specs = (
        P("qry", None),
        P(("doc", "qry"), None),
        P(("doc", "qry")),
        P(),
        P(None, ("doc", "qry")),
    )
    out_specs = (P(None, ("doc", "qry")), P("qry"))
    return jax.shard_map(
        on_device, mesh=mesh, in_specs=in_specs, out_specs=out_specs, check_vma=False
    )
```

```python
import functools
import random

import jax
import jax.numpy as jnp
from jax import lax
from jax.experimental import pallas as pl
from jax.experimental.pallas import tpu as pltpu
from jax.sharding import PartitionSpec as P

MAXP = 16
LANES = 128
SUBLANES = 8
PACKED = 16
ORDER_SEED = 25
TOTALS_SEED = 35

score_scale = 0.03125
very_negative = -1e30

VMEM = pl.BlockSpec(memory_space=pltpu.VMEM)
HBM = pl.BlockSpec(memory_space=pltpu.HBM)
NT = (((1,), (1,)), ((), ()))


def place_in(order, index):
    out = jnp.zeros(index.shape, jnp.int32)
    for place, entry in enumerate(order):
        out = jnp.where(index == entry, place, out)
    return out


def rolled(array, columns):
    if columns == 0:
        return array
    return jnp.concatenate([array[:, columns:], array[:, :columns]], axis=1)


def from_own(array, core, rows_dev, query_groups):
    out = array
    for mine in range(1, query_groups):
        out = jnp.where(core == mine, rolled(array, mine * rows_dev), out)
    return out


def from_first(array, core, rows_dev, query_groups):
    out = array
    for mine in range(1, query_groups):
        out = jnp.where(core == mine, rolled(array, (query_groups - mine) * rows_dev), out)
    return out


def dot_nt(a, b):
    return lax.dot_general(a, b, NT, preferred_element_type=jnp.float32)


def before_kernel(
    sizes, passages_hbm, own_hbm, route_hbm, pattern_hbm, teacher_hbm,
    passages_ref, own_ref, place_ref, ids_ref, weights_ref, notes_ref,
    route_ref, pattern_ref, teacher_ref, passages_sem, small_sem,
):
    doc_count, query_groups, capacity, table_rows, rows_dev, order = sizes
    rows = passages_ref.shape[0]
    pairs = [
        (route_hbm, route_ref),
        (pattern_hbm, pattern_ref),
        (teacher_hbm, teacher_ref),
        (own_hbm, own_ref),
    ]
    small = [
        pltpu.make_async_copy(source, target, small_sem.at[k])
        for k, (source, target) in enumerate(pairs)
    ]
    large = pltpu.make_async_copy(passages_hbm, passages_ref, passages_sem)
    small[0].start()
    large.start()
    for copy in small[1:]:
        copy.start()
    core = lax.axis_index("qry")
    group_id = lax.axis_index("doc") * query_groups + core

    small[0].wait()
    route = route_ref[...]
    owner = route // table_rows
    target = place_in(order, owner // query_groups).astype(jnp.float32)
    slot = (route - owner * table_rows).astype(jnp.float32)
    down = lax.broadcasted_iota(jnp.int32, (rows, rows), 0)
    across = lax.broadcasted_iota(jnp.int32, (rows, rows), 1)

    def as_column(row):
        row = jnp.broadcast_to(row, (rows, rows))
        return jnp.sum(jnp.where(down == across, row, 0.0), axis=1, keepdims=True)

    earlier = (as_column(target) == target) & (down < across)
    position = jnp.sum(jnp.where(earlier, 1.0, 0.0), axis=0, keepdims=True)
    placing = target * capacity + position
    outgoing = lax.broadcasted_iota(jnp.int32, (doc_count * capacity, rows), 0).astype(jnp.float32)
    place_ref[...] = jnp.where(outgoing == placing, 1.0, 0.0).astype(place_ref.dtype)
    columns = ids_ref.shape[1]
    mine = place_in(order, jnp.full((1, 1), lax.axis_index("doc"), jnp.int32)) * capacity
    arriving = as_column(position) + mine.astype(jnp.float32)
    number = as_column(slot) + 1.0
    row = lax.broadcasted_iota(jnp.int32, (ids_ref.shape[0], rows), 0)
    column = lax.broadcasted_iota(jnp.int32, (rows, columns), 1).astype(jnp.float32)
    ids = jnp.zeros(ids_ref.shape, jnp.float32)
    for line in range(-(-doc_count * capacity // columns)):
        goes = ((row // SUBLANES).astype(jnp.float32) == target) & (row % SUBLANES == line)
        goes = jnp.where(goes, 1.0, 0.0).astype(jnp.bfloat16)
        here = jnp.where(column + float(line * columns) == arriving, number, 0.0)
        ids += jnp.dot(goes, here.astype(jnp.bfloat16), preferred_element_type=jnp.float32)
    ids_ref[...] = ids

    small[1].wait()
    small[2].wait()
    all_queries = rows_dev * query_groups
    lane = lax.broadcasted_iota(jnp.int32, (1, all_queries), 1)
    own = lax.broadcasted_iota(jnp.int32, pattern_ref.shape, 1) == group_id
    flags = jnp.sum(jnp.where(own, pattern_ref[...], 0), axis=1, keepdims=True)
    active = jnp.zeros((1, all_queries), jnp.float32)
    for block in range(query_groups):
        inside = (lane >= block * rows_dev) & (lane < (block + 1) * rows_dev)
        flag = jnp.broadcast_to(flags[block : block + 1], (1, all_queries))
        active = jnp.where(inside & (flag > 0), 1.0, active)
    active = from_own(active, core, rows_dev, query_groups)
    teacher = from_own(teacher_ref[...], core, rows_dev, query_groups)
    peak = jnp.max(teacher, axis=0, keepdims=True)
    weights = jnp.exp(teacher - peak)
    weight_sum = jnp.sum(weights, axis=0, keepdims=True)
    weights = weights / weight_sum
    weights_ref[...] = weights
    notes_ref[0:1, :] = jnp.where(active > 0.0, peak + jnp.log(weight_sum), very_negative)
    notes_ref[1:2, :] = jnp.sum(weights * teacher, axis=0, keepdims=True)
    notes_ref[2:3, :] = active
    notes_ref[3:, :] = jnp.zeros((notes_ref.shape[0] - 3, all_queries), jnp.float32)
    small[3].wait()
    large.wait()


def pack_kernel(passages_ref, place_ref, ids_ref, *refs):
    query_refs, out_ref = refs[:-1], refs[-1]
    doc_count, block_rows, columns = out_ref.shape
    capacity = block_rows - SUBLANES
    queries = jnp.concatenate([part[...] for part in query_refs], axis=0)
    logits = dot_nt(passages_ref[...], queries) * score_scale
    high = logits.astype(jnp.bfloat16)
    low = (logits - high.astype(jnp.float32)).astype(jnp.bfloat16)
    placed = jnp.dot(
        place_ref[...], jnp.concatenate([high, low], axis=1), preferred_element_type=jnp.float32
    )
    out_ref[:, :capacity, :] = placed.reshape(doc_count, capacity, columns).astype(out_ref.dtype)
    ids = ids_ref[...].reshape(doc_count, SUBLANES, columns)
    out_ref[:, capacity:, :] = ids.astype(out_ref.dtype)


def pool_kernel(rows_dev, query_groups, arrived_ref, weights_ref, notes_ref, scores_ref, lines_ref):
    doc_dev, all_queries = weights_ref.shape
    table_rows = doc_dev * MAXP
    doc_count, block_rows, columns = arrived_ref.shape
    capacity = block_rows - SUBLANES
    slots = doc_count * capacity
    ids = jnp.sum(arrived_ref[:, capacity:, :].astype(jnp.float32), axis=0)
    lines = [ids[line : line + 1] for line in range(-(-slots // columns))]
    id_row = jnp.concatenate(lines, axis=1)[:, :slots]
    shape = (MAXP, doc_dev, slots)
    wanted = lax.broadcasted_iota(jnp.int32, shape, 0) + lax.broadcasted_iota(jnp.int32, shape, 1) * MAXP
    wanted = wanted.reshape(table_rows, slots).astype(jnp.float32) + 1.0
    chosen = jnp.where(wanted == id_row, 1.0, 0.0).astype(jnp.bfloat16)
    arrived = arrived_ref[:, :capacity, :].reshape(slots, columns)
    table = jnp.dot(chosen, arrived, preferred_element_type=jnp.float32)
    scores = table[:, :all_queries] + table[:, all_queries:]
    document = lax.broadcasted_iota(jnp.int32, (doc_dev, slots), 0).astype(jnp.float32)
    held = jnp.floor((id_row - 1.0) * (1.0 / MAXP)) == document
    count = jnp.sum(jnp.where(held, 1.0, 0.0), axis=1, keepdims=True)
    count = jnp.broadcast_to(count, (doc_dev, all_queries))
    scores = scores.reshape(MAXP, doc_dev, all_queries)
    places = [jnp.where(count > place, scores[place], very_negative) for place in range(MAXP)]
    highest = functools.reduce(jnp.maximum, places)
    total = functools.reduce(jnp.add, [jnp.exp(place - highest) for place in places])
    pooled = highest + jnp.log(total)
    active = notes_ref[2:3, :] > 0.0
    scores_ref[...] = jnp.where(active, pooled, 0.0)
    peak = jnp.max(highest, axis=0, keepdims=True)
    student = peak + jnp.log(jnp.sum(total * jnp.exp(highest - peak), axis=0, keepdims=True))
    student = jnp.where(active, student, very_negative)
    mean = notes_ref[1:2, :] - jnp.sum(weights_ref[...] * pooled, axis=0, keepdims=True)
    teacher = notes_ref[0:1, :]
    row = lax.broadcasted_iota(jnp.int32, lines_ref.shape, 0)
    lines = jnp.zeros(lines_ref.shape, jnp.float32)
    for block in range(query_groups):
        part = slice(block * rows_dev, (block + 1) * rows_dev)
        line = jnp.concatenate(
            [
                student[:, part],
                teacher[:, part],
                mean[:, part],
                jnp.zeros((1, lines_ref.shape[1] - 3 * rows_dev), jnp.float32),
            ],
            axis=1,
        )
        lines = jnp.where(row == block, jnp.broadcast_to(line, lines_ref.shape), lines)
    lines_ref[...] = lines


def order_kernel(rows_dev, query_groups, scores_ref, out_ref):
    out_ref[...] = from_first(scores_ref[...], lax.axis_index("qry"), rows_dev, query_groups)


def joined(parts, rows_dev):
    peak = functools.reduce(jnp.maximum, parts)
    weights = [jnp.exp(part - peak) for part in parts]
    total = functools.reduce(jnp.add, weights)
    moved = [rolled(weight, weight.shape[1] - rows_dev) for weight in weights + [total]]
    weighted = functools.reduce(jnp.add, [w * part for w, part in zip(moved, parts)])
    lane = lax.broadcasted_iota(jnp.int32, peak.shape, 1)
    totals = peak + jnp.log(total)
    return jnp.where(lane < 2 * rows_dev, totals, weighted / moved[-1])


def spread_kernel(first_place, rows_dev, *refs):
    line_refs, out_ref = refs[:-1], refs[-1]
    sources = len(line_refs)
    place = lax.broadcasted_iota(jnp.int32, out_ref.shape, 0)
    crossed = jnp.where(place == first_place, 1, 0)
    here = jnp.where(lax.axis_index("doc") == 0, 1, 0)
    part = (crossed - here + sources) % sources
    out = jnp.zeros(out_ref.shape, jnp.float32)
    for ahead in range(sources):
        held = [(ahead - k) % sources for k in range(sources)]
        line = joined([lines[h : h + 1, :] for lines, h in zip(line_refs, held)], rows_dev)
        out = jnp.where(part == ahead, jnp.broadcast_to(line, out_ref.shape), out)
    out_ref[...] = out


def merge_kernel(rows_dev, parts_ref, out_ref):
    parts = parts_ref[...]
    peak = jnp.max(parts, axis=0, keepdims=True)
    weights = jnp.exp(parts - peak)
    total = jnp.sum(weights, axis=0, keepdims=True)
    moved = jnp.concatenate([weights[:, -rows_dev:], weights[:, :-rows_dev]], axis=1)
    weighted = jnp.sum(moved * parts, axis=0, keepdims=True)
    totals = peak + jnp.log(total)
    columns = [slice(k * rows_dev, (k + 1) * rows_dev) for k in range(3)]
    out_ref[...] = (
        weighted[:, columns[2]] / total[:, columns[1]] - totals[:, columns[1]] + totals[:, columns[0]]
    )


def call(kernel, out_shape, in_specs, scratch=(), **cost):
    several = isinstance(out_shape, (list, tuple))
    return pl.pallas_call(
        kernel,
        out_shape=out_shape,
        in_specs=in_specs,
        out_specs=[VMEM] * len(out_shape) if several else VMEM,
        scratch_shapes=scratch,
        compiler_params=pltpu.CompilerParams(vmem_limit_bytes=16 * 1024 * 1024),
        cost_estimate=pl.CostEstimate(**cost) if cost else None,
    )


def crossed_groups(order, query_groups):
    return [
        [doc * query_groups + (core + (doc == 0)) % query_groups for doc in order]
        for core in range(query_groups)
    ]


def shuffled_from(first, size, seed=ORDER_SEED):
    others = [k for k in range(size) if k != first]
    return [first] + random.Random(seed).sample(others, size - 1)


def from_others(array, query_groups):
    return [
        lax.ppermute(array, "qry", [((i + k) % query_groups, i) for i in range(query_groups)])
        for k in range(1, query_groups)
    ]


def on_device(queries, passages, passage_route, pattern, teacher):
    doc_count = lax.axis_size("doc")
    query_groups = lax.axis_size("qry")
    rows_dev, width = queries.shape
    rows = passages.shape[0]
    all_queries, doc_dev = teacher.shape
    table_rows = doc_dev * MAXP
    capacity = -(-table_rows // (doc_count * PACKED)) * PACKED
    last_doc = doc_count - 1
    order = shuffled_from(last_doc, doc_count, TOTALS_SEED)
    route_order = shuffled_from(last_doc - doc_count // 4, doc_count)
    f32, bf16 = jnp.float32, jnp.bfloat16
    shaped = jax.ShapeDtypeStruct

    others = from_others(queries, query_groups)
    held, own, place, ids, weights, notes = call(
        functools.partial(
            before_kernel,
            (doc_count, query_groups, capacity, table_rows, rows_dev, route_order),
        ),
        [
            shaped((rows, width), bf16),
            shaped((rows_dev, width), bf16),
            shaped((doc_count * capacity, rows), bf16),
            shaped((doc_count * SUBLANES, 2 * all_queries), f32),
            shaped((doc_dev, all_queries), f32),
            shaped((SUBLANES, all_queries), f32),
        ],
        [HBM] * 5,
        [
            pltpu.VMEM((1, rows), jnp.int32),
            pltpu.VMEM(pattern.shape, jnp.int32),
            pltpu.VMEM((doc_dev, all_queries), f32),
            pltpu.SemaphoreType.DMA(()),
            pltpu.SemaphoreType.DMA((4,)),
        ],
        flops=doc_count * capacity * rows,
        bytes_accessed=2 * (rows + rows_dev) * width,
        transcendentals=0,
    )(
        *[
            pltpu.with_memory_space_constraint(array, pltpu.HBM)
            for array in (passages, queries, passage_route.reshape(1, rows), pattern, teacher.T)
        ]
    )
    outgoing = call(
        pack_kernel,
        shaped((doc_count, capacity + SUBLANES, 2 * all_queries), bf16),
        [VMEM] * (4 + len(others)),
    )(held, place, ids, own, *others)
    arrived = lax.all_to_all(
        outgoing,
        "doc",
        split_axis=0,
        concat_axis=0,
        axis_index_groups=[route_order],
        tiled=True,
    )
    line = -(-3 * rows_dev // LANES) * LANES
    lines_rows = -(-query_groups // SUBLANES) * SUBLANES
    doc_scores, lines = call(
        functools.partial(pool_kernel, rows_dev, query_groups),
        [shaped((doc_dev, all_queries), f32), shaped((lines_rows, line), f32)],
        [VMEM, VMEM, VMEM],
    )(arrived, weights, notes)
    received = from_others(lines, query_groups)
    doc_scores = call(
        functools.partial(order_kernel, rows_dev, query_groups),
        shaped((doc_dev, all_queries), f32),
        [VMEM],
    )(doc_scores)
    doc_scores, received = lax.optimization_barrier((doc_scores, received))
    partials = call(
        functools.partial(spread_kernel, order.index(0), rows_dev),
        shaped((doc_count, line), f32),
        [VMEM] * query_groups,
    )(lines, *received)
    everyone = lax.all_to_all(
        partials,
        ("doc", "qry"),
        split_axis=0,
        concat_axis=0,
        axis_index_groups=crossed_groups(order, query_groups),
        tiled=True,
    )
    divergence = call(
        functools.partial(merge_kernel, rows_dev), shaped((1, rows_dev), f32), [VMEM]
    )(everyone)
    return (doc_scores.T, divergence.reshape(rows_dev))


def solution(mesh):
    in_specs = (
        P("qry", None),
        P(("doc", "qry"), None),
        P(("doc", "qry")),
        P(),
        P(None, ("doc", "qry")),
    )
    out_specs = (P(None, ("doc", "qry")), P("qry"))
    return jax.shard_map(
        on_device, mesh=mesh, in_specs=in_specs, out_specs=out_specs, check_vma=False
    )
```
